128 devices in a mesh: gx: 4 (over z), gy: 4 (over y), gz: 8 (over x, core).
Axes of the slice: x: 4, y: 4, z: 4, core: 2. Of those that a mesh axis runs over, the one named last changes fastest.
Arguments:
- coarse_state: float32 [64, 10, 64, 1024], P('gx', None, 'gy', 'gz'), may hold values from -6 to 6
- fine_state: float32 [2048, 16, 10, 256], P(('gx', 'gy', 'gz')), may hold values from -6 to 6
- flux_jacobians: float32 [3, 10, 10], replicated, may hold values from -2 to 2
- fine_owner: int32 [1024], replicated, may hold values from 0 to 2047, as said below
- fine_offset: int32 [1024, 3], replicated, may hold values from 1 to 7
Outputs:
- coarse_out: float32 [64, 10, 64, 1024], P('gx', None, 'gy', 'gz')
- fine_out: float32 [2048, 16, 10, 256], P(('gx', 'gy', 'gz'))
The draws below stay inside these ranges and needn't reach their ends.
Inputs may be any that keep to these rules, and one draw needn't show every extreme that they name: `fine_owner`: every fine box has a slot of its own. The 8 fine boxes over one device's coarse boxes are held by 8 different devices with that device's gz index, and the fine boxes that one device holds lie over coarse boxes of different devices. A device's fine boxes fill its first slots, and in every gx-gy plane one device holds 16.
All inputs are finite; a program needn't handle non-finite values.
Results may differ from the reference program's by a relative error of at most 0.0003.
Values sent between devices are 32-bit elements; how exact they have to be, the bound alone decides.
No kernel may reach another device: no remote copies, remote signals or barrier semaphores. Data moves between devices by JAX's collectives and lax.ppermute only.
A program may use at most 256 MiB of HBM per device.

```python
import jax
import jax.numpy as jnp
from jax import lax

F = 10
B = 16
BOXES = 8
SUBSTEPS = 2
H = 8
FSLOTS = 16
NX = 64
NY = 64
NZ = 1024
NFINE = 1024
GROUP = 16
LINES = 8
N_GX = 4
N_GY = 4
N_GZ = 8
DEVICES = 128


def draw_fine_owner(key, part):
    key = jax.random.fold_in(key, 23)
    sub_keys = jax.random.split(key, 3)
    position = jnp.arange(GROUP, dtype=jnp.int32)
    within = jnp.arange(BOXES, dtype=jnp.int32)
    heavy_source = position[:, None] < 2 * BOXES
    others = 1 + (position[:, None] + jnp.where(heavy_source, within[None, :] - 1, within[None, :])) % (GROUP - 1)
    target = jnp.where(heavy_source & (within[None, :] == 0), 0, others).astype(jnp.int32)
    holder_order = jax.vmap(lambda sub_key: jax.random.permutation(sub_key, GROUP))(jax.random.split(sub_keys[0], LINES)).astype(jnp.int32)
    source_order = jax.vmap(lambda sub_key: jax.random.permutation(sub_key, GROUP))(jax.random.split(sub_keys[1], LINES)).astype(jnp.int32)
    box_order = jax.vmap(lambda sub_key: jax.random.permutation(sub_key, BOXES))(jax.random.split(sub_keys[2], LINES * GROUP)).astype(jnp.int32)
    box_order = box_order.reshape(LINES, GROUP, BOXES)
    shuffled = jnp.take_along_axis(jnp.broadcast_to(target[None], (LINES, GROUP, BOXES)), box_order, axis=2)
    holder_member = jnp.take_along_axis(holder_order, shuffled.reshape(LINES, GROUP * BOXES), axis=1).reshape(LINES, GROUP, BOXES)
    inverse = jnp.argsort(source_order, axis=1).astype(jnp.int32)
    by_member = jnp.take_along_axis(holder_member, jnp.broadcast_to(inverse[:, :, None], (LINES, GROUP, BOXES)), axis=1)
    sends_to = jnp.any(by_member[:, :, :, None] == position[None, None, None, :], axis=2).astype(jnp.int32)
    earlier = jnp.cumsum(sends_to, axis=1) - sends_to
    slot_index = jnp.take_along_axis(earlier, by_member, axis=2)
    line_index = jnp.arange(LINES, dtype=jnp.int32)
    owner_value = (by_member * LINES + line_index[:, None, None]) * FSLOTS + slot_index
    return jnp.transpose(owner_value, (1, 0, 2)).reshape(-1).astype(jnp.int32)


def plant(array, rng, low, top_value):
    longest = array.shape.index(max(array.shape))
    spots = []
    for shift in (0, 1):
        where = [jax.random.randint(jax.random.fold_in(rng, axis), (), 0, length) for axis, length in enumerate(array.shape)]
        where[longest] = (where[longest] + shift) % array.shape[longest]
        spots.append(tuple(where))
    return array.at[spots[0]].set(low).at[spots[1]].set(top_value)


def shard_levels(stream_key, dims, cuts, low, largest):
    loudness = 1.0
    for dim, parts in cuts:
        heights = jax.random.uniform(jax.random.fold_in(jax.random.fold_in(stream_key, 6), dim), (parts,), jnp.float32, low / len(cuts), largest / len(cuts))
        loudness = loudness * jnp.repeat(jnp.exp(heights), dims[dim] // parts).reshape((-1,) + (1,) * (len(dims) - 1 - dim))
    return loudness


def centred(key, dims, width, bound, shards=(), held_as=jnp.bfloat16):
    values = jax.random.normal(key, dims, jnp.float32) * width
    if len(shards) > 0:
        values = shard_levels(key, dims, shards, -0.22, 0.18) * values
    return jnp.clip(values, min=-bound, max=bound).astype(held_as)


def setup_inputs(seed: int = 0) -> dict:
    key_of = jax.random.split(jax.random.key(seed), 6)
    return {
        "coarse_state": centred(key_of[0], (NX, F, NY, NZ), 1.0, 6.0, ((0, 4), (2, 4), (3, 8)), jnp.float32),
        "fine_state": centred(key_of[1], (DEVICES * FSLOTS, B, F, B * B), 1.0, 6.0, ((0, 128),), jnp.float32),
        "flux_jacobians": centred(key_of[2], (3, F, F), F ** -0.5, 2.0, (), jnp.float32),
        "fine_owner": draw_fine_owner(jax.random.fold_in(key_of[5], 71), 0),
        "fine_offset": plant(jax.random.randint(key_of[4], (NFINE, 3), 1, B // 2), jax.random.fold_in(key_of[4], 1), 1, (B // 2) - 1).astype(jnp.int32),
    }


courant = 0.25


def padded_change(padded, flux_jacobians):
    center = padded[1:-1, :, 1:-1, 1:-1]
    neighbours = ((padded[2:, :, 1:-1, 1:-1], padded[:-2, :, 1:-1, 1:-1]),
                  (padded[1:-1, :, 2:, 1:-1], padded[1:-1, :, :-2, 1:-1]),
                  (padded[1:-1, :, 1:-1, 2:], padded[1:-1, :, 1:-1, :-2]))
    change = jnp.zeros(center.shape, center.dtype)
    for direction, (forward_cells, backward_cells) in enumerate(neighbours):
        flux_term = jnp.einsum('gf,xfyz->xgyz', flux_jacobians[direction], forward_cells - backward_cells, precision=lax.Precision.HIGHEST)
        change = change + 0.5 * flux_term - 0.5 * (forward_cells - 2.0 * center + backward_cells)
    return change


def upsample(coarse_cells):
    doubled = jnp.repeat(coarse_cells, 2, axis=0)
    doubled = jnp.repeat(doubled, 2, axis=2)
    return jnp.repeat(doubled, 2, axis=3)


def box_corner(box_id, fine_offset):
    device = box_id // BOXES
    within = box_id % BOXES
    plane_x = device // (N_GY * N_GZ)
    plane_y = (device // N_GZ) % N_GY
    plane_z = device % N_GZ
    start_x = plane_x * B + fine_offset[box_id, 0]
    start_y = plane_y * B + fine_offset[box_id, 1]
    start_z = (plane_z * BOXES + within) * B + fine_offset[box_id, 2]
    return start_x, start_y, start_z


def reference(coarse_state, fine_state, flux_jacobians, fine_owner, fine_offset):
    wrapped = jnp.pad(coarse_state, ((1, 1), (0, 0), (1, 1), (1, 1)), mode="wrap")
    block_starts = jnp.arange(N_GX, dtype=jnp.int32) * B

    def coarse_block(row_start):
        return padded_change(lax.dynamic_slice_in_dim(wrapped, row_start, B + 2, 0), flux_jacobians)

    changes = lax.map(coarse_block, block_starts)
    coarse_new = coarse_state - courant * changes.reshape(coarse_state.shape)
    zero_index = jnp.zeros((), jnp.int32)

    def advance_box(box_id):
        start_x, start_y, start_z = box_corner(box_id, fine_offset)
        corner = (start_x - 1, zero_index, start_y - 1, start_z - 1)
        extent = (H + 2, F, H + 2, H + 2)
        shell_old = lax.dynamic_slice(coarse_state, corner, extent)
        shell_new = lax.dynamic_slice(coarse_new, corner, extent)
        fine_box = fine_state[fine_owner[box_id]].reshape(B, F, B, B)
        for substep in range(SUBSTEPS):
            weight_new = substep / SUBSTEPS
            ghost_cells = upsample((1.0 - weight_new) * shell_old + weight_new * shell_new)[1:-1, :, 1:-1, 1:-1]
            padded = ghost_cells.at[1:-1, :, 1:-1, 1:-1].set(fine_box)
            fine_box = fine_box - courant * padded_change(padded, flux_jacobians)
        averages = 0.125 * jnp.sum(fine_box.reshape(H, 2, F, H, 2, H, 2), axis=(1, 4, 6))
        return fine_box.reshape(B, F, B * B), averages

    box_ids = jnp.arange(NFINE, dtype=jnp.int32)
    fine_boxes, averages = lax.map(advance_box, box_ids)
    fine_out = jnp.zeros_like(fine_state).at[fine_owner].set(fine_boxes)

    def place_average(coarse, box_entry):
        box_id, average = box_entry
        start_x, start_y, start_z = box_corner(box_id, fine_offset)
        return lax.dynamic_update_slice(coarse, average, (start_x, zero_index, start_y, start_z)), None

    coarse_out, unused = lax.scan(place_average, coarse_new, (box_ids, averages))
    return coarse_out, fine_out
```

```python
import functools

import jax
import jax.numpy as jnp
import ml_dtypes
import numpy as np
from jax import lax
from jax.experimental import pallas as pl
from jax.experimental.pallas import tpu as pltpu
from jax.sharding import PartitionSpec as P

F = 10
B = 16
BOXES = 8
H = 8
FSLOTS = 16
LINES = 8
GROUP = 16
ROWS = F * B
HALF = F * H
F32 = jnp.float32
BF16 = jnp.bfloat16
VMEM_LIMIT = 40 * 1024 * 1024


def dot(a, b):
    return jnp.dot(a, b, preferred_element_type=F32)


def split(v):
    hi = v.astype(BF16)
    return hi, (v - hi.astype(F32)).astype(BF16)


def lanes_of(shape):
    return lax.broadcasted_iota(jnp.int32, shape, len(shape) - 1)


def expand_constants():
    rows = np.zeros((ROWS, 16), np.float32)
    for g in range(F):
        rows[g * B : (g + 1) * B, g] = 1
    first = np.zeros((128, 512), np.float32)
    second = np.zeros((128, 512), np.float32)
    mask_first = np.zeros((ROWS, 512), np.float32)
    mask_second = np.zeros((ROWS, 512), np.float32)
    for f in range(F):
        for x in range(B):
            first[f, f * B + x] = 1
            second[16 + f, f * B + x] = 1
            first[32 + f, ROWS + f * B + x] = 1
            first[48 + f, 2 * ROWS + f * B + x] = 1
            for g in range(F):
                if x > 0:
                    mask_first[g * B + x - 1, f * B + x] = 1
                if x < B - 1:
                    mask_second[g * B + x + 1, f * B + x] = 1
                mask_first[g * B + x, ROWS + f * B + x] = 1
                mask_first[g * B + x, 2 * ROWS + f * B + x] = 1
        first[16 + f, 3 * ROWS + f] = 1
        first[f, 3 * ROWS + 16 + f] = 1
        mask_first[0::B, 3 * ROWS + f] = 1
        mask_first[B - 1 :: B, 3 * ROWS + 16 + f] = 1
    return [a.astype(ml_dtypes.bfloat16) for a in (rows, first, second, mask_first, mask_second)]


def fine_constants():
    up = np.zeros((ROWS, 2 * HALF), np.float32)
    pair = np.zeros((HALF, 2 * ROWS), np.float32)
    for f in range(F):
        for x in range(B):
            for part in range(2):
                up[f * B + x, part * HALF + f * H + x // 2] = 1
                pair[f * H + x // 2, part * ROWS + f * B + x] = 0.125
    ghost = np.zeros((128, 768), np.float32)
    face = np.zeros((128, 256), np.float32)
    mean = np.zeros((512, 128), np.float32)
    for part in range(2):
        for t in range(2):
            for j in range(B):
                low, col = part * 64 + t * 32 + j // 2, t * 384
                ghost[low, col + j] = 1
                ghost[low + 8, col + 112 + j] = 1
                ghost[low + 16, col + 128 + j * B] = 1
                ghost[low + 24, col + 128 + j * B + B - 1] = 1
        for y in range(B):
            for z in range(B):
                face[part * 64 + y // 2 * H + z // 2, y * B + z] = 1
                mean[part * 256 + y * B + z, y // 2 * H + z // 2] = 1
    return [a.astype(ml_dtypes.bfloat16) for a in (up, pair, ghost, face, mean)]


def coefficients_kernel(jac_ref, rows_ref, first_ref, second_ref, mask1_ref, mask2_ref, out_ref, pad_ref):
    pad_ref[...] = jnp.zeros(pad_ref.shape, F32)
    for d in range(3):
        pad_ref[d, 0:F, 0:F] = jac_ref[d]
    shape = (16, 128)
    row = lax.broadcasted_iota(jnp.int32, shape, 0)
    eye = jnp.where((row == lanes_of(shape)) & (row < F), 0.125, 0.0).astype(F32)
    scaled = [0.125 * pad_ref[d] for d in range(3)]
    for level, (s, a, b) in enumerate(((1, 0, 2), (0, 1, 2))):
        coef = (
            (eye - scaled[s])
            + pltpu.roll(eye + scaled[s], 16, 1)
            - pltpu.roll(scaled[a], 32, 1)
            - pltpu.roll(scaled[b], 48, 1)
        )
        for part, value in enumerate(split(coef)):
            wide1 = dot(value, first_ref[...]).astype(BF16)
            wide2 = dot(value, second_ref[...]).astype(BF16)
            both = dot(rows_ref[...], wide1) * mask1_ref[...].astype(F32) + dot(
                rows_ref[...], wide2
            ) * mask2_ref[...].astype(F32)
            out_ref[level, part] = both.astype(BF16)


def faces_kernel(coarse_ref, x_lo, x_hi, y_lo, y_hi, z_lo, z_hi):
    x_lo[...] = coarse_ref[0:ROWS, :]
    x_hi[...] = coarse_ref[(B - 1) * ROWS : B * ROWS, :]
    for x in range(B):
        y_lo[x * F : x * F + F, :] = coarse_ref[pl.ds(x * ROWS, F, stride=B), :]
        y_hi[x * F : x * F + F, :] = coarse_ref[pl.ds(x * ROWS + B - 1, F, stride=B), :]
    lane = lanes_of((ROWS, 128))
    low = jnp.zeros((ROWS, 128), F32)
    high = jnp.zeros((ROWS, 128), F32)
    for x in range(B):
        plane = coarse_ref[x * ROWS : (x + 1) * ROWS, :]
        low = jnp.where(lane == x, pltpu.roll(plane, x, 1), low)
        high = jnp.where(lane == x, pltpu.roll(plane, x + 1, 1), high)
    z_lo[...] = low
    z_hi[...] = high


def coarse_kernel(
    place_ref, coarse_ref, x_lo, x_hi, y_lo, y_hi, z_lo, z_hi, coef_ref, new_ref, out_ref, mid_ref, hi_ref, lo_ref
):
    lane = lanes_of((ROWS, 128))
    ghost_zero = jnp.zeros((16 - F, 128), F32)
    for pair in range(B // 2):
        rest = []
        for side in range(2):
            x = 2 * pair + side
            cols = slice(side * 128, side * 128 + 128)
            p = coarse_ref[x * ROWS : (x + 1) * ROWS, :]
            xm = coarse_ref[(x - 1) * ROWS : x * ROWS, :] if x > 0 else x_lo[...]
            xp = coarse_ref[(x + 1) * ROWS : (x + 2) * ROWS, :] if x < B - 1 else x_hi[...]
            zm = jnp.where(lane == 0, pltpu.roll(z_lo[...], (128 - x) % 128, 1), pltpu.roll(p, 1, 1))
            zp = jnp.where(lane == 127, pltpu.roll(z_hi[...], 127 - x, 1), pltpu.roll(p, 127, 1))
            ghosts = jnp.concatenate(
                [y_lo[x * F : x * F + F, :], ghost_zero, y_hi[x * F : x * F + F, :], ghost_zero], axis=0
            )
            for at, value in ((0, p), (ROWS, xp - xm), (2 * ROWS, zp - zm), (3 * ROWS, ghosts)):
                hi, lo = split(value)
                hi_ref[at : at + value.shape[0], cols] = hi
                lo_ref[at : at + value.shape[0], cols] = lo
            rest.append(0.25 * p + 0.125 * ((xp + xm) + (zp + zm)))
        total = dot(coef_ref[0, 0], hi_ref[...]) + dot(coef_ref[0, 0], lo_ref[...]) + dot(coef_ref[0, 1], hi_ref[...])
        for side in range(2):
            x = 2 * pair + side
            new = rest[side] + total[:, side * 128 : side * 128 + 128]
            new_ref[x * ROWS : (x + 1) * ROWS, :] = new
            mid_ref[x * ROWS : (x + 1) * ROWS, :] = 0.5 * (coarse_ref[x * ROWS : (x + 1) * ROWS, :] + new)

    lane8 = lanes_of((8, 128))
    within = lane8 % 32
    base = jnp.where(within < 16, within % 8, jnp.where(within < 24, -1, 8))
    window = lane8 % 8

    def box(w, _):
        member = place_ref[w]
        ox, oy, oz = place_ref[8 + 3 * w], place_ref[9 + 3 * w], place_ref[10 + 3 * w]
        z0 = w * B + oz
        pick = base + z0
        pick_x = window + z0
        corner = ox * ROWS + oy - 1
        for f in range(F):
            acc = jnp.zeros((8, 128), F32)
            for t, ref in enumerate((coarse_ref, mid_ref)):
                for y in range(H + 2):
                    rows = ref[pl.ds(corner + f * B + y, H, stride=ROWS), :]
                    moved = jnp.take_along_axis(rows, pick, axis=1, mode="promise_in_bounds")
                    if y == 0:
                        put = (lane8 >= 32 * t) & (lane8 < 32 * t + 8)
                    elif y == H + 1:
                        put = (lane8 >= 32 * t + 8) & (lane8 < 32 * t + 16)
                    else:
                        put = (lane8 == 32 * t + 15 + y) | (lane8 == 32 * t + 23 + y)
                    acc = jnp.where(put, moved, acc)
            out_ref[member, f * 8 : f * 8 + 8, :] = acc
        for t, ref in enumerate((coarse_ref, mid_ref)):
            for side, x in enumerate((ox - 1, ox + H)):
                first = jnp.zeros((8, 128), F32)
                second = jnp.zeros((8, 128), F32)
                for y in range(H):
                    put = (lane8 >= 64 + y * 8) & (lane8 < 72 + y * 8)
                    at = x * ROWS + oy + y
                    rows = ref[pl.ds(at, 8, stride=B), :]
                    first = jnp.where(put, jnp.take_along_axis(rows, pick_x, axis=1, mode="promise_in_bounds"), first)
                    tail = jnp.concatenate(
                        [ref[pl.ds(at + 8 * B, F - 8, stride=B), :], jnp.zeros((16 - F, 128), F32)], axis=0
                    )
                    second = jnp.where(
                        put, jnp.take_along_axis(tail, pick_x, axis=1, mode="promise_in_bounds"), second
                    )
                at = (2 * t + side) * 16
                old = out_ref[member, at : at + 16, :]
                out_ref[member, at : at + 16, :] = jnp.where(
                    lanes_of((16, 128)) < 64, old, jnp.concatenate([first, second], axis=0)
                )
        return 0

    lax.fori_loop(0, BOXES, box, 0)


def fine_kernel(
    source_ref, fine_ref, arrived_ref, coef_ref, up_ref, pair_ref, ghost_ref, face_ref, mean_ref, out_ref, back_ref,
    hi_ref, lo_ref, wide_ref
):
    slot = pl.program_id(0)
    source = source_ref[slot]

    @pl.when(source < 0)
    def _():
        out_ref[...] = jnp.zeros(out_ref.shape, F32)

    @pl.when(source >= 0)
    def _():
        message = arrived_ref[source]
        m_hi, m_lo = split(message)
        lifted = dot(up_ref[...], jnp.concatenate([m_hi, m_lo], axis=0))
        lane = lanes_of((ROWS, 128))
        hi = lifted.astype(BF16).astype(F32)
        mixed = jnp.where(lane < 64, hi, pltpu.roll(lifted - hi, 64, 1)).astype(BF16)
        wide_ref[...] = dot(mixed, ghost_ref[...])
        top = message[0:64, :]
        hi = top.astype(BF16).astype(F32)
        mixed = jnp.where(lanes_of((64, 128)) < 64, pltpu.roll(top - hi, 64, 1), hi).astype(BF16)
        x_ghosts = dot(mixed, face_ref[...])
        p = fine_ref[0].reshape(ROWS, 256)
        column = lane % B
        for t in range(2):
            at = 384 * t
            gy = wide_ref[:, at : at + 128]
            gz_a = wide_ref[:, at + 128 : at + 256]
            gz_b = wide_ref[:, at + 256 : at + 384]
            a, b = p[:, 0:128], p[:, 128:256]
            a_up, b_up = pltpu.roll(a, 112, 1), pltpu.roll(b, 112, 1)
            a_down, b_down = pltpu.roll(a, 16, 1), pltpu.roll(b, 16, 1)
            yp = (jnp.where(lane < 112, a_up, b_up), jnp.where(lane < 112, b_up, gy))
            ym = (jnp.where(lane < 16, gy, a_down), jnp.where(lane < 16, a_down, b_down))
            zp = (
                jnp.where(column == B - 1, gz_a, pltpu.roll(a, 127, 1)),
                jnp.where(column == B - 1, gz_b, pltpu.roll(b, 127, 1)),
            )
            zm = (
                jnp.where(column == 0, gz_a, pltpu.roll(a, 1, 1)),
                jnp.where(column == 0, gz_b, pltpu.roll(b, 1, 1)),
            )
            rest = []
            for k, v in enumerate((a, b)):
                cols = slice(128 * k, 128 * k + 128)
                for start, value in ((0, v), (ROWS, yp[k] - ym[k]), (2 * ROWS, zp[k] - zm[k])):
                    v_hi, v_lo = split(value)
                    hi_ref[start : start + ROWS, cols] = v_hi
                    lo_ref[start : start + ROWS, cols] = v_lo
                rest.append(0.25 * v + 0.125 * ((yp[k] + ym[k]) + (zp[k] + zm[k])))
            g_hi, g_lo = split(x_ghosts[32 * t : 32 * t + 32, :])
            hi_ref[3 * ROWS : 3 * ROWS + 32, :] = g_hi
            lo_ref[3 * ROWS : 3 * ROWS + 32, :] = g_lo
            total = (
                dot(coef_ref[1, 0], hi_ref[...]) + dot(coef_ref[1, 0], lo_ref[...]) + dot(coef_ref[1, 1], hi_ref[...])
            )
            p = jnp.concatenate(rest, axis=1) + total
        out_ref[0] = p.reshape(F, B, 256)
        p_hi, p_lo = split(p)
        paired = dot(pair_ref[...], jnp.concatenate([p_hi, p_lo], axis=0))
        q_hi, q_lo = split(paired)
        means = dot(jnp.concatenate([q_hi, q_lo], axis=1), mean_ref[...])
        back_ref[source] = jnp.where(
            lanes_of((HALF // 2, 128)) < 64, means[: HALF // 2], pltpu.roll(means[HALF // 2 :], 64, 1)
        )


def place_kernel(place_ref, new_ref, back_ref, out_ref):
    out_ref[...] = new_ref[...]
    lane = lanes_of((8, 128))

    def box(w, _):
        member = place_ref[w]
        ox, oy, oz = place_ref[8 + 3 * w], place_ref[9 + 3 * w], place_ref[10 + 3 * w]
        z0 = w * B + oz
        inside = (lane >= z0) & (lane < z0 + H)
        pick = jnp.where(inside, lane - z0, 0)
        corner = ox * ROWS + oy
        for f in range(F):
            tile = back_ref[member, f % 5 * 8 : f % 5 * 8 + 8, :]
            for y in range(H):
                moved = jnp.take_along_axis(tile, pick + (f // 5 * 64 + y * 8), axis=1, mode="promise_in_bounds")
                rows = pl.ds(corner + f * B + y, H, stride=ROWS)
                out_ref[rows, :] = jnp.where(inside, moved, out_ref[rows, :])
        return 0

    lax.fori_loop(0, BOXES, box, 0)


def vmem():
    return pl.BlockSpec(memory_space=pltpu.VMEM)


def smem():
    return pl.BlockSpec(memory_space=pltpu.SMEM)


def call(kernel, ins, outs, scratch=()):
    return pl.pallas_call(
        kernel,
        in_specs=ins,
        out_specs=[vmem() for _ in outs],
        out_shape=[jax.ShapeDtypeStruct(*out) for out in outs],
        scratch_shapes=list(scratch),
        compiler_params=pltpu.CompilerParams(vmem_limit_bytes=VMEM_LIMIT),
    )


def local(coarse_state, fine_state, flux_jacobians, fine_owner, fine_offset):
    device = lax.axis_index(("gx", "gy", "gz"))
    rows = coarse_state.reshape(B * ROWS, 128)
    fine_rows = jnp.transpose(fine_state, (0, 2, 1, 3))

    my_member = lax.dynamic_slice_in_dim(fine_owner, device * BOXES, BOXES) // (FSLOTS * LINES)
    my_offset = lax.dynamic_slice_in_dim(fine_offset, device * BOXES, BOXES, 0)
    place = jnp.concatenate([my_member, my_offset.reshape(-1)])
    slot_ids = device * FSLOTS + jnp.arange(FSLOTS, dtype=jnp.int32)
    members = jnp.arange(fine_owner.shape[0], dtype=jnp.int32) // (BOXES * LINES)
    source = jnp.max(jnp.where(fine_owner[None, :] == slot_ids[:, None], members[None, :], -1), axis=1)

    consts = expand_constants()
    coef = call(
        coefficients_kernel,
        [vmem()] * 6,
        [((2, 2, ROWS, 512), BF16)],
        [pltpu.VMEM((3, 16, 128), F32)],
    )(flux_jacobians, *consts)[0]

    face = ((ROWS, 128), F32)
    x_first, x_last, y_first, y_last, z_first, z_last = call(faces_kernel, [vmem()], [face] * 6)(rows)

    def from_below(value, axis):
        n = lax.axis_size(axis)
        return lax.ppermute(value, axis, [(i, (i + 1) % n) for i in range(n)])

    def from_above(value, axis):
        n = lax.axis_size(axis)
        return lax.ppermute(value, axis, [((i + 1) % n, i) for i in range(n)])

    halo = (
        from_below(x_last, "gx"),
        from_above(x_first, "gx"),
        from_below(y_last, "gy"),
        from_above(y_first, "gy"),
        from_below(z_last, "gz"),
        from_above(z_first, "gz"),
    )
    new, outgoing = call(
        coarse_kernel,
        [smem()] + [vmem()] * 8,
        [((B * ROWS, 128), F32), ((GROUP, HALF, 128), F32)],
        [pltpu.VMEM((B * ROWS, 128), F32), pltpu.VMEM((512, 256), BF16), pltpu.VMEM((512, 256), BF16)],
    )(place, rows, *halo, coef)
    arrived = lax.all_to_all(outgoing, ("gx", "gy"), split_axis=0, concat_axis=0, tiled=True)

    whole = lambda shape: pl.BlockSpec(shape, lambda i: (0,) * len(shape))
    block = pl.BlockSpec((1, F, B, 256), lambda i: (i, 0, 0, 0))
    fconsts = fine_constants()
    fine_new, returning = pl.pallas_call(
        fine_kernel,
        grid=(FSLOTS,),
        in_specs=[smem(), block, whole((GROUP, HALF, 128)), whole((2, 2, ROWS, 512))]
        + [whole(c.shape) for c in fconsts],
        out_specs=[block, whole((GROUP, HALF // 2, 128))],
        out_shape=[
            jax.ShapeDtypeStruct((FSLOTS, F, B, 256), F32),
            jax.ShapeDtypeStruct((GROUP, HALF // 2, 128), F32),
        ],
        scratch_shapes=[
            pltpu.VMEM((512, 256), BF16),
            pltpu.VMEM((512, 256), BF16),
            pltpu.VMEM((ROWS, 768), F32),
        ],
        compiler_params=pltpu.CompilerParams(vmem_limit_bytes=VMEM_LIMIT),
    )(source, fine_rows, arrived, coef, *fconsts)
    came_back = lax.all_to_all(returning, ("gx", "gy"), split_axis=0, concat_axis=0, tiled=True)

    coarse_out = call(place_kernel, [smem(), vmem(), vmem()], [((B * ROWS, 128), F32)])(place, new, came_back)[0]
    return coarse_out.reshape(coarse_state.shape), jnp.transpose(fine_new, (0, 2, 1, 3))


def solution(mesh):
    in_specs = (P("gx", None, "gy", "gz"), P(("gx", "gy", "gz"), None, None, None), P(), P(), P())
    out_specs = (P("gx", None, "gy", "gz"), P(("gx", "gy", "gz"), None, None, None))
    return jax.shard_map(local, mesh=mesh, in_specs=in_specs, out_specs=out_specs, check_vma=False)
```

```python
import functools

import jax
import jax.numpy as jnp
import ml_dtypes
import numpy as np
from jax import lax
from jax.experimental import pallas as pl
from jax.experimental.pallas import tpu as pltpu
from jax.sharding import PartitionSpec as P

F = 10
B = 16
BOXES = 8
H = 8
FSLOTS = 16
LINES = 8
GROUP = 16
ROWS = F * B
HALF = F * H
F32 = jnp.float32
BF16 = jnp.bfloat16
VMEM_LIMIT = 60 * 1024 * 1024
BATCH = 8


def dot(a, b):
    return jnp.dot(a, b, preferred_element_type=F32)


def split(v):
    hi = v.astype(BF16)
    return hi, (v - hi.astype(F32)).astype(BF16)


def lanes_of(shape):
    return lax.broadcasted_iota(jnp.int32, shape, len(shape) - 1)


def expand_constants():
    rows = np.zeros((ROWS, 16), np.float32)
    for g in range(F):
        rows[g * B : (g + 1) * B, g] = 1
    first = np.zeros((128, 512), np.float32)
    second = np.zeros((128, 512), np.float32)
    mask_first = np.zeros((ROWS, 512), np.float32)
    mask_second = np.zeros((ROWS, 512), np.float32)
    for f in range(F):
        for x in range(B):
            first[f, f * B + x] = 1
            second[16 + f, f * B + x] = 1
            first[32 + f, ROWS + f * B + x] = 1
            first[48 + f, 2 * ROWS + f * B + x] = 1
            for g in range(F):
                if x > 0:
                    mask_first[g * B + x - 1, f * B + x] = 1
                if x < B - 1:
                    mask_second[g * B + x + 1, f * B + x] = 1
                mask_first[g * B + x, ROWS + f * B + x] = 1
                mask_first[g * B + x, 2 * ROWS + f * B + x] = 1
        first[16 + f, 3 * ROWS + f] = 1
        first[f, 3 * ROWS + 16 + f] = 1
        mask_first[0::B, 3 * ROWS + f] = 1
        mask_first[B - 1 :: B, 3 * ROWS + 16 + f] = 1
    rows = np.pad(rows, ((0, 0), (0, 512 - 16)))
    return np.concatenate([rows, mask_first, mask_second, first, second]).astype(ml_dtypes.bfloat16)


def fine_constants():
    up = np.zeros((ROWS, 2 * HALF), np.float32)
    pair = np.zeros((HALF, 2 * ROWS), np.float32)
    for f in range(F):
        for x in range(B):
            for part in range(2):
                up[f * B + x, part * HALF + f * H + x // 2] = 1
                pair[f * H + x // 2, part * ROWS + f * B + x] = 0.125
    ghost = np.zeros((128, 768), np.float32)
    face = np.zeros((128, 256), np.float32)
    mean = np.zeros((512, 128), np.float32)
    for part in range(2):
        for t in range(2):
            for j in range(B):
                low, col = part * 64 + t * 32 + j // 2, t * 384
                ghost[low, col + j] = 1
                ghost[low + 8, col + 112 + j] = 1
                ghost[low + 16, col + 128 + j * B] = 1
                ghost[low + 24, col + 128 + j * B + B - 1] = 1
        for y in range(B):
            for z in range(B):
                face[part * 64 + y // 2 * H + z // 2, y * B + z] = 1
                mean[part * 256 + y * B + z, y // 2 * H + z // 2] = 1
    return [a.astype(ml_dtypes.bfloat16) for a in (up, pair, ghost, face, mean)]


def coefficients_kernel(jac_ref, const_ref, out_ref, pad_ref):
    pad_ref[...] = jnp.zeros(pad_ref.shape, F32)
    for d in range(3):
        pad_ref[d, 0:F, 0:F] = jac_ref[d]
    shape = (16, 128)
    row = lax.broadcasted_iota(jnp.int32, shape, 0)
    eye = jnp.where((row == lanes_of(shape)) & (row < F), 0.125, 0.0).astype(F32)
    scaled = [0.125 * pad_ref[d] for d in range(3)]
    for level, (s, a, b) in enumerate(((1, 0, 2), (0, 1, 2))):
        coef = (
            (eye - scaled[s])
            + pltpu.roll(eye + scaled[s], 16, 1)
            - pltpu.roll(scaled[a], 32, 1)
            - pltpu.roll(scaled[b], 48, 1)
        )
        for part, value in enumerate(split(coef)):
            wide1 = dot(value, const_ref[3 * ROWS : 3 * ROWS + 128, :]).astype(BF16)
            wide2 = dot(value, const_ref[3 * ROWS + 128 : 3 * ROWS + 256, :]).astype(BF16)
            rows = const_ref[0:ROWS, 0:128]
            pad = jnp.zeros((112, 512), BF16)
            both = dot(rows, jnp.concatenate([wide1, pad], axis=0)) * const_ref[ROWS : 2 * ROWS, :].astype(F32)
            both += dot(rows, jnp.concatenate([wide2, pad], axis=0)) * const_ref[2 * ROWS : 3 * ROWS, :].astype(F32)
            out_ref[level, part] = both.astype(BF16)


def faces_kernel(coarse_ref, x_lo, x_hi, y_lo, y_hi, z_lo, z_hi):
    x_lo[...] = coarse_ref[0:ROWS, :]
    x_hi[...] = coarse_ref[(B - 1) * ROWS : B * ROWS, :]
    for x in range(B):
        y_lo[x * F : x * F + F, :] = coarse_ref[pl.ds(x * ROWS, F, stride=B), :]
        y_hi[x * F : x * F + F, :] = coarse_ref[pl.ds(x * ROWS + B - 1, F, stride=B), :]
    lane = lanes_of((ROWS, 128))
    low = jnp.zeros((ROWS, 128), F32)
    high = jnp.zeros((ROWS, 128), F32)
    for x in range(B):
        plane = coarse_ref[x * ROWS : (x + 1) * ROWS, :]
        low = jnp.where(lane == x, pltpu.roll(plane, x, 1), low)
        high = jnp.where(lane == x, pltpu.roll(plane, x + 1, 1), high)
    z_lo[...] = low
    z_hi[...] = high


def product(coef_ref, level, hi_ref, lo_ref, total_ref):
    both = dot(coef_ref[level].reshape(2 * ROWS, 512), hi_ref[...])
    total_ref[...] = both[:ROWS] + both[ROWS:] + dot(coef_ref[level, 0], lo_ref[...])


def put_parts(hi_ref, lo_ref, cols, parts):
    for at, value in parts:
        hi, lo = split(value)
        hi_ref[at : at + value.shape[0], cols] = hi
        lo_ref[at : at + value.shape[0], cols] = lo


def coarse_kernel(
    place_ref, coarse_ref, x_lo, x_hi, y_lo, y_hi, z_lo, z_hi, coef_ref, new_ref, out_ref, mid_ref, hi_ref, lo_ref,
    rest_ref, total_ref
):
    lane = lanes_of((B, 128))
    ghost_zero = jnp.zeros((16 - F, 128), F32)
    for pair in range(B // 2):
        for side in range(2):
            x = 2 * pair + side
            cols = slice(side * 128, side * 128 + 128)
            for f in range(F):
                row = slice(f * B, f * B + B)
                here = x * ROWS + f * B
                p = coarse_ref[here : here + B, :]
                xm = coarse_ref[here - ROWS : here - ROWS + B, :] if x > 0 else x_lo[row, :]
                xp = coarse_ref[here + ROWS : here + ROWS + B, :] if x < B - 1 else x_hi[row, :]
                zm = jnp.where(lane == 0, pltpu.roll(z_lo[row, :], (128 - x) % 128, 1), pltpu.roll(p, 1, 1))
                zp = jnp.where(lane == 127, pltpu.roll(z_hi[row, :], 127 - x, 1), pltpu.roll(p, 127, 1))
                put_parts(
                    hi_ref.at[pair],
                    lo_ref.at[pair],
                    cols,
                    ((f * B, p), (ROWS + f * B, xp - xm), (2 * ROWS + f * B, zp - zm)),
                )
                rest_ref[pair, row, cols] = 0.25 * p + 0.125 * ((xp + xm) + (zp + zm))
            low = jnp.concatenate([y_lo[x * F : x * F + F, :], ghost_zero], axis=0)
            high = jnp.concatenate([y_hi[x * F : x * F + F, :], ghost_zero], axis=0)
            put_parts(hi_ref.at[pair], lo_ref.at[pair], cols, ((3 * ROWS, low), (3 * ROWS + 16, high)))
    for pair in range(B // 2):
        product(coef_ref, 0, hi_ref.at[pair], lo_ref.at[pair], total_ref.at[pair])
    for pair in range(B // 2):
        for side in range(2):
            x = 2 * pair + side
            cols = slice(side * 128, side * 128 + 128)
            for f in range(F):
                row = slice(f * B, f * B + B)
                here = slice(x * ROWS + f * B, x * ROWS + f * B + B)
                new = rest_ref[pair, row, cols] + total_ref[pair, row, cols]
                new_ref[here, :] = new
                mid_ref[here, :] = 0.5 * (coarse_ref[here, :] + new)

    lane8 = lanes_of((8, 128))
    within = lane8 % 32
    base = jnp.where(within < 16, within % 8, jnp.where(within < 24, -1, 8))
    window = lane8 % 8

    def box(w, _):
        member = place_ref[w]
        ox, oy, oz = place_ref[8 + 3 * w], place_ref[9 + 3 * w], place_ref[10 + 3 * w]
        z0 = w * B + oz
        pick = base + z0
        pick_x = window + z0
        corner = ox * ROWS + oy - 1
        for f in range(F):
            acc = jnp.zeros((8, 128), F32)
            for t, ref in enumerate((coarse_ref, mid_ref)):
                for y in range(H + 2):
                    rows = ref[pl.ds(corner + f * B + y, H, stride=ROWS), :]
                    moved = jnp.take_along_axis(rows, pick, axis=1, mode="promise_in_bounds")
                    if y == 0:
                        put = (lane8 >= 32 * t) & (lane8 < 32 * t + 8)
                    elif y == H + 1:
                        put = (lane8 >= 32 * t + 8) & (lane8 < 32 * t + 16)
                    else:
                        put = (lane8 == 32 * t + 15 + y) | (lane8 == 32 * t + 23 + y)
                    acc = jnp.where(put, moved, acc)
            out_ref[member, f * 8 : f * 8 + 8, :] = acc
        for t, ref in enumerate((coarse_ref, mid_ref)):
            for side, x in enumerate((ox - 1, ox + H)):
                first = jnp.zeros((8, 128), F32)
                second = jnp.zeros((8, 128), F32)
                for y in range(H):
                    put = (lane8 >= 64 + y * 8) & (lane8 < 72 + y * 8)
                    at = x * ROWS + oy + y
                    rows = ref[pl.ds(at, 8, stride=B), :]
                    first = jnp.where(put, jnp.take_along_axis(rows, pick_x, axis=1, mode="promise_in_bounds"), first)
                    tail = jnp.concatenate(
                        [ref[pl.ds(at + 8 * B, F - 8, stride=B), :], jnp.zeros((16 - F, 128), F32)], axis=0
                    )
                    second = jnp.where(
                        put, jnp.take_along_axis(tail, pick_x, axis=1, mode="promise_in_bounds"), second
                    )
                at = (2 * t + side) * 16
                old = out_ref[member, at : at + 16, :]
                out_ref[member, at : at + 16, :] = jnp.where(
                    lanes_of((16, 128)) < 64, old, jnp.concatenate([first, second], axis=0)
                )
        return 0

    lax.fori_loop(0, BOXES, box, 0, unroll=2)


def fine_kernel(
    source_ref, fine_ref, arrived_ref, coef_ref, up_ref, pair_ref, ghost_ref, face_ref, mean_ref, out_ref, back_ref,
    hi_ref, lo_ref, wide_ref, rest_ref, total_ref, value_ref, face_out_ref, parts_ref, mixed_ref, back_scratch
):
    first_slot = pl.program_id(0) * BATCH
    sources = [source_ref[first_slot + k] for k in range(BATCH)]

    @pl.when(sources[0] < 0)
    def _():
        out_ref[...] = jnp.zeros(out_ref.shape, F32)

    @pl.when(sources[0] >= 0)
    def _():
        lane = lanes_of((B, 128))
        column = lane % B
        for k in range(BATCH):
            message = arrived_ref.at[jnp.maximum(sources[k], 0)]
            for at in range(0, HALF, 16):
                value = message[at : at + 16, :]
                hi, lo = split(value)
                parts_ref[k, at : at + 16, :] = hi
                parts_ref[k, HALF + at : HALF + at + 16, :] = lo
                if at < 64:
                    hi = hi.astype(F32)
                    mixed_ref[k, ROWS + at : ROWS + at + 16, :] = jnp.where(
                        lane < 64, pltpu.roll(value - hi, 64, 1), hi
                    ).astype(BF16)
        for k in range(BATCH):
            lifted = dot(up_ref[...], parts_ref[k])
            for f in range(F):
                value = lifted[f * B : f * B + B]
                hi = value.astype(BF16).astype(F32)
                mixed_ref[k, f * B : f * B + B, :] = jnp.where(lane < 64, hi, pltpu.roll(value - hi, 64, 1)).astype(
                    BF16
                )
        for k in range(BATCH):
            wide_ref[k] = dot(mixed_ref[k, 0:ROWS, :], ghost_ref[...])
            face_out_ref[k] = dot(mixed_ref[k, ROWS : ROWS + 64, :], face_ref[...])
        for t in range(2):
            at = 384 * t
            for k in range(BATCH):
                for f in range(F):
                    row = slice(f * B, f * B + B)
                    if t == 0:
                        a, b = fine_ref[k, f, :, 0:128], fine_ref[k, f, :, 128:256]
                    else:
                        a, b = value_ref[k, row, 0:128], value_ref[k, row, 128:256]
                    gy = wide_ref[k, row, at : at + 128]
                    gz_a = wide_ref[k, row, at + 128 : at + 256]
                    gz_b = wide_ref[k, row, at + 256 : at + 384]
                    a_up, b_up = pltpu.roll(a, 112, 1), pltpu.roll(b, 112, 1)
                    a_down, b_down = pltpu.roll(a, 16, 1), pltpu.roll(b, 16, 1)
                    yp = (jnp.where(lane < 112, a_up, b_up), jnp.where(lane < 112, b_up, gy))
                    ym = (jnp.where(lane < 16, gy, a_down), jnp.where(lane < 16, a_down, b_down))
                    zp = (
                        jnp.where(column == B - 1, gz_a, pltpu.roll(a, 127, 1)),
                        jnp.where(column == B - 1, gz_b, pltpu.roll(b, 127, 1)),
                    )
                    zm = (
                        jnp.where(column == 0, gz_a, pltpu.roll(a, 1, 1)),
                        jnp.where(column == 0, gz_b, pltpu.roll(b, 1, 1)),
                    )
                    for h, v in enumerate((a, b)):
                        cols = slice(128 * h, 128 * h + 128)
                        put_parts(
                            hi_ref.at[k],
                            lo_ref.at[k],
                            cols,
                            ((f * B, v), (ROWS + f * B, yp[h] - ym[h]), (2 * ROWS + f * B, zp[h] - zm[h])),
                        )
                        rest_ref[k, row, cols] = 0.25 * v + 0.125 * ((yp[h] + ym[h]) + (zp[h] + zm[h]))
                put_parts(
                    hi_ref.at[k], lo_ref.at[k], slice(None), ((3 * ROWS, face_out_ref[k, 32 * t : 32 * t + 32, :]),)
                )
            for k in range(BATCH):
                product(coef_ref, 1, hi_ref.at[k], lo_ref.at[k], total_ref.at[k])
            for k in range(BATCH):
                for f in range(F):
                    row = slice(f * B, f * B + B)
                    value = rest_ref[k, row, :] + total_ref[k, row, :]
                    if t == 0:
                        value_ref[k, row, :] = value
                    else:
                        out_ref[k, f] = jnp.where(sources[k] >= 0, value, 0.0)
                        hi, lo = split(value)
                        hi_ref[k, row, :] = hi
                        hi_ref[k, ROWS + f * B : ROWS + f * B + B, :] = lo
        for k in range(BATCH):
            paired = dot(pair_ref[...], hi_ref[k, 0 : 2 * ROWS, :])
            hi, lo = split(paired)
            means = dot(jnp.concatenate([hi, lo], axis=1), mean_ref[...])
            back_scratch[k] = jnp.where(
                lanes_of((HALF // 2, 128)) < 64, means[: HALF // 2], pltpu.roll(means[HALF // 2 :], 64, 1)
            )

    for k in range(BATCH):

        @pl.when(sources[k] >= 0)
        def _():
            back_ref[sources[k]] = back_scratch[k]


def place_kernel(place_ref, new_ref, back_ref, out_ref):
    out_ref[...] = new_ref[...]
    lane = lanes_of((8, 128))

    def box(w, _):
        member = place_ref[w]
        ox, oy, oz = place_ref[8 + 3 * w], place_ref[9 + 3 * w], place_ref[10 + 3 * w]
        z0 = w * B + oz
        inside = (lane >= z0) & (lane < z0 + H)
        pick = jnp.where(inside, lane - z0, 0)
        corner = ox * ROWS + oy
        for f in range(F):
            tile = back_ref[member, f % 5 * 8 : f % 5 * 8 + 8, :]
            rows = [pl.ds(corner + f * B + y, H, stride=ROWS) for y in range(H)]
            before = [out_ref[r, :] for r in rows]
            for y in range(H):
                moved = jnp.take_along_axis(tile, pick + (f // 5 * 64 + y * 8), axis=1, mode="promise_in_bounds")
                out_ref[rows[y], :] = jnp.where(inside, moved, before[y])
        return 0

    lax.fori_loop(0, BOXES, box, 0)


def whole(shape):
    return pl.BlockSpec(shape, lambda i: (0,) * len(shape))


def smem():
    return pl.BlockSpec(memory_space=pltpu.SMEM)


def call(kernel, operands, outs, scratch=(), grid=(1,), blocks=(), out_blocks=()):
    blocks, out_blocks = dict(blocks), dict(out_blocks)
    return pl.pallas_call(
        kernel,
        grid=grid,
        in_specs=[blocks.get(i) or (smem() if a.ndim == 1 else whole(a.shape)) for i, a in enumerate(operands)],
        out_specs=[out_blocks.get(i) or whole(shape) for i, (shape, _) in enumerate(outs)],
        out_shape=[jax.ShapeDtypeStruct(*out) for out in outs],
        scratch_shapes=list(scratch),
        compiler_params=pltpu.CompilerParams(vmem_limit_bytes=VMEM_LIMIT),
    )(*operands)


def local(coarse_state, fine_state, flux_jacobians, fine_owner, fine_offset):
    device = lax.axis_index(("gx", "gy", "gz"))
    rows = coarse_state.reshape(B * ROWS, 128)
    fine_rows = jnp.transpose(fine_state, (0, 2, 1, 3))

    my_member = lax.dynamic_slice_in_dim(fine_owner, device * BOXES, BOXES) // (FSLOTS * LINES)
    my_offset = lax.dynamic_slice_in_dim(fine_offset, device * BOXES, BOXES, 0)
    place = jnp.concatenate([my_member, my_offset.reshape(-1)])
    slot_ids = device * FSLOTS + jnp.arange(FSLOTS, dtype=jnp.int32)
    members = jnp.arange(fine_owner.shape[0], dtype=jnp.int32) // (BOXES * LINES)
    source = jnp.max(jnp.where(fine_owner[None, :] == slot_ids[:, None], members[None, :], -1), axis=1)

    coef = call(
        coefficients_kernel,
        (flux_jacobians, expand_constants()),
        [((2, 2, ROWS, 512), BF16)],
        [pltpu.VMEM((3, 16, 128), F32)],
    )[0]

    face = ((ROWS, 128), F32)
    x_first, x_last, y_first, y_last, z_first, z_last = call(faces_kernel, (rows,), [face] * 6)

    def from_below(value, axis):
        n = lax.axis_size(axis)
        return lax.ppermute(value, axis, [(i, (i + 1) % n) for i in range(n)])

    def from_above(value, axis):
        n = lax.axis_size(axis)
        return lax.ppermute(value, axis, [((i + 1) % n, i) for i in range(n)])

    halo = (
        from_below(x_last, "gx"),
        from_above(x_first, "gx"),
        from_below(y_last, "gy"),
        from_above(y_first, "gy"),
        from_below(z_last, "gz"),
        from_above(z_first, "gz"),
    )
    new, outgoing = call(
        coarse_kernel,
        (place, rows, *halo, coef),
        [((B * ROWS, 128), F32), ((GROUP, HALF, 128), F32)],
        [pltpu.VMEM((B * ROWS, 128), F32)]
        + [pltpu.VMEM((B // 2, 512, 256), BF16)] * 2
        + [pltpu.VMEM((B // 2, ROWS, 256), F32)] * 2,
    )
    arrived = lax.all_to_all(outgoing, ("gx", "gy"), split_axis=0, concat_axis=0, tiled=True)

    block = pl.BlockSpec((BATCH, F, B, 256), lambda i: (i, 0, 0, 0))
    fine_new, returning = call(
        fine_kernel,
        (source, fine_rows, arrived, coef, *fine_constants()),
        [((FSLOTS, F, B, 256), F32), ((GROUP, HALF // 2, 128), F32)],
        [pltpu.VMEM((BATCH, 512, 256), BF16)] * 2
        + [pltpu.VMEM((BATCH, ROWS, 768), F32)]
        + [pltpu.VMEM((BATCH, ROWS, 256), F32)] * 3
        + [
            pltpu.VMEM((BATCH, 64, 256), F32),
            pltpu.VMEM((BATCH, 2 * HALF, 128), BF16),
            pltpu.VMEM((BATCH, ROWS + 64, 128), BF16),
            pltpu.VMEM((BATCH, HALF // 2, 128), F32),
        ],
        grid=(FSLOTS // BATCH,),
        blocks=((1, block),),
        out_blocks=((0, block),),
    )
    came_back = lax.all_to_all(returning, ("gx", "gy"), split_axis=0, concat_axis=0, tiled=True)

    coarse_out = call(place_kernel, (place, new, came_back), [((B * ROWS, 128), F32)])[0]
    return coarse_out.reshape(coarse_state.shape), jnp.transpose(fine_new, (0, 2, 1, 3))


def solution(mesh):
    in_specs = (P("gx", None, "gy", "gz"), P(("gx", "gy", "gz"), None, None, None), P(), P(), P())
    out_specs = (P("gx", None, "gy", "gz"), P(("gx", "gy", "gz"), None, None, None))
    return jax.shard_map(local, mesh=mesh, in_specs=in_specs, out_specs=out_specs, check_vma=False)
```

```python
import functools

import jax
import jax.numpy as jnp
import ml_dtypes
import numpy as np
from jax import lax
from jax.experimental import pallas as pl
from jax.experimental.pallas import tpu as pltpu
from jax.sharding import PartitionSpec as P

F = 10
B = 16
BOXES = 8
H = 8
FSLOTS = 16
LINES = 8
GROUP = 16
ROWS = F * B
HALF = F * H
F32 = jnp.float32
BF16 = jnp.bfloat16
MIB = 1024 * 1024
PITCH = ROWS + 8
BATCH = 8


def dot(a, b):
    return jnp.dot(a, b, preferred_element_type=F32)


def split(v):
    hi = v.astype(BF16)
    return hi, (v - hi.astype(F32)).astype(BF16)


def lanes_of(shape):
    return lax.broadcasted_iota(jnp.int32, shape, len(shape) - 1)


CONST = {
    "ghost": (slice(0, 128), slice(0, 768)),
    "up": (slice(128, 288), slice(0, 160)),
    "pair": (slice(128, 208), slice(256, 576)),
    "face": (slice(288, 416), slice(0, 256)),
    "mean": (slice(128, 384), slice(640, 768)),
}


def fine_constants():
    up = np.zeros((ROWS, 2 * HALF), np.float32)
    pair = np.zeros((HALF, 2 * ROWS), np.float32)
    for f in range(F):
        for x in range(B):
            for part in range(2):
                up[f * B + x, part * HALF + f * H + x // 2] = 1
                pair[f * H + x // 2, part * ROWS + f * B + x] = 0.125
    ghost = np.zeros((128, 768), np.float32)
    face = np.zeros((128, 256), np.float32)
    mean = np.zeros((256, 128), np.float32)
    for part in range(2):
        for t in range(2):
            for j in range(B):
                low, col = part * 64 + t * 32 + j // 2, t * 384
                ghost[low, col + j] = 1
                ghost[low + 8, col + 112 + j] = 1
                ghost[low + 16, col + 128 + j * B] = 1
                ghost[low + 24, col + 128 + j * B + B - 1] = 1
        for y in range(B):
            for z in range(B):
                face[part * 64 + y // 2 * H + z // 2, y * B + z] = 1
                mean[y * B + z, y // 2 * H + z // 2] = 1
    every = np.zeros((416, 768), np.float32)
    for name, value in (("ghost", ghost), ("up", up), ("pair", pair), ("face", face), ("mean", mean)):
        rows, cols = CONST[name]
        every[rows, cols] = value
    return every.astype(ml_dtypes.bfloat16)


def device_index():
    return (lax.axis_index("gx") * lax.axis_size("gy") + lax.axis_index("gy")) * lax.axis_size("gz") + lax.axis_index("gz")


def box_place(owner_ref, offset_ref, w):
    box = device_index() * BOXES + w
    return (owner_ref[box] // (FSLOTS * LINES), *(offset_ref[d, box] for d in range(3)))


def coefficients(jac_ref, pad_ref, outs):
    pad_ref[...] = jnp.zeros(pad_ref.shape, F32)
    for d in range(3):
        for g in range(F):
            pad_ref[d, g : g + 1, 0:F] = jac_ref[g, d : d + 1, :]
    row, lane = (lax.broadcasted_iota(jnp.int32, (128, 128), d) for d in range(2))
    eye = jnp.where((row[:16] == lane[:16]) & (row[:16] < F), 0.125, 0.0).astype(F32)
    scaled = [0.125 * pad_ref[d] for d in range(3)]
    row, col = (lax.broadcasted_iota(jnp.int32, (128, 512), d) for d in range(2))
    block, inner = col // ROWS, col % ROWS // B
    ghost = 3 * ROWS
    target = jnp.where(col < ghost, inner + jnp.where(block == 0, 0, 16 + 16 * block), (col + 16) % 32)
    one = lambda cond: jnp.where(cond, 1.0, 0.0).astype(F32)
    first = one(row == target).astype(BF16)
    second = one((col < ROWS) & (row == 16 + inner)).astype(BF16)
    row, col = (lax.broadcasted_iota(jnp.int32, (ROWS, 512), d) for d in range(2))
    here, there = row % B, col % B
    edge = jnp.where(col < ghost + 16, 0, B - 1)
    distance = jnp.where(col < ROWS, there - here - 1, jnp.where(col < ghost, there - here, here - edge))
    mask_first = one(distance == 0)
    mask_second = one((col < ROWS) & (there + 1 == here))
    row, col = (lax.broadcasted_iota(jnp.int32, (ROWS, 128), d) for d in range(2))
    rows = one(row // B == col).astype(BF16)
    pad = jnp.zeros((112, 512), BF16)
    for (s, a, b), out in zip(((1, 0, 2), (0, 1, 2)), outs):
        coef = (
            (eye - scaled[s])
            + pltpu.roll(eye + scaled[s], 16, 1)
            - pltpu.roll(scaled[a], 32, 1)
            - pltpu.roll(scaled[b], 48, 1)
        )
        for part, value in enumerate(split(coef)):
            wide1 = jnp.concatenate([dot(value, first).astype(BF16), pad], axis=0)
            wide2 = jnp.concatenate([dot(value, second).astype(BF16), pad], axis=0)
            out[part] = (dot(rows, wide1) * mask_first + dot(rows, wide2) * mask_second).astype(BF16)


def faces_kernel(coarse_ref, x_lo, x_hi, y_lo, y_hi, z_lo, z_hi):
    x_lo[...] = coarse_ref[0:ROWS, :]
    x_hi[...] = coarse_ref[(B - 1) * ROWS : B * ROWS, :]
    for x in range(B):
        y_lo[x * F : x * F + F, :] = coarse_ref[pl.ds(x * ROWS, F, stride=B), :]
        y_hi[x * F : x * F + F, :] = coarse_ref[pl.ds(x * ROWS + B - 1, F, stride=B), :]
    lane = lanes_of((ROWS, 128))
    low = jnp.zeros((ROWS, 128), F32)
    high = jnp.zeros((ROWS, 128), F32)
    for x in range(B):
        plane = coarse_ref[x * ROWS : (x + 1) * ROWS, :]
        low = jnp.where(lane == x, pltpu.roll(plane, x, 1), low)
        high = jnp.where(lane == x, pltpu.roll(plane, x + 1, 1), high)
    z_lo[...] = low
    z_hi[...] = high


def product(coef_ref, hi_ref, lo_ref, total_ref):
    both = dot(coef_ref[...].reshape(2 * ROWS, 512), hi_ref[...])
    total_ref[...] = both[:ROWS] + both[ROWS:] + dot(coef_ref[0], lo_ref[...])


def put_parts(hi_ref, lo_ref, cols, parts):
    for at, value in parts:
        hi, lo = split(value)
        hi_ref[at : at + value.shape[0], cols] = hi
        lo_ref[at : at + value.shape[0], cols] = lo


def coarse_kernel(
    owner_ref, offset_ref, coarse_ref, x_lo, x_hi, y_lo, y_hi, z_lo, z_hi, jac_ref, new_ref, out_ref, fine_coef_ref, old_ref,
    mid_ref, hi_ref, lo_ref, rest_ref, total_ref, coef_ref, pad_ref
):
    coefficients(jac_ref, pad_ref, (coef_ref, fine_coef_ref))
    lane = lanes_of((B, 128))
    ghost_zero = jnp.zeros((16 - F, 128), F32)
    for pair in range(B // 2):
        for side in range(2):
            x = 2 * pair + side
            cols = slice(side * 128, side * 128 + 128)
            for f in range(F):
                row = slice(f * B, f * B + B)
                here = x * ROWS + f * B
                p = coarse_ref[here : here + B, :]
                xm = coarse_ref[here - ROWS : here - ROWS + B, :] if x > 0 else x_lo[row, :]
                xp = coarse_ref[here + ROWS : here + ROWS + B, :] if x < B - 1 else x_hi[row, :]
                zm = jnp.where(lane == 0, pltpu.roll(z_lo[row, :], (128 - x) % 128, 1), pltpu.roll(p, 1, 1))
                zp = jnp.where(lane == 127, pltpu.roll(z_hi[row, :], 127 - x, 1), pltpu.roll(p, 127, 1))
                put_parts(
                    hi_ref.at[pair],
                    lo_ref.at[pair],
                    cols,
                    ((f * B, p), (ROWS + f * B, xp - xm), (2 * ROWS + f * B, zp - zm)),
                )
                rest_ref[pair, row, cols] = 0.25 * p + 0.125 * ((xp + xm) + (zp + zm))
                old_ref[x * PITCH + f * B : x * PITCH + f * B + B, :] = p
            low = jnp.concatenate([y_lo[x * F : x * F + F, :], ghost_zero], axis=0)
            high = jnp.concatenate([y_hi[x * F : x * F + F, :], ghost_zero], axis=0)
            put_parts(hi_ref.at[pair], lo_ref.at[pair], cols, ((3 * ROWS, low), (3 * ROWS + 16, high)))
    for pair in range(B // 2):
        product(coef_ref, hi_ref.at[pair], lo_ref.at[pair], total_ref.at[pair])
    for pair in range(B // 2):
        for side in range(2):
            x = 2 * pair + side
            cols = slice(side * 128, side * 128 + 128)
            for f in range(F):
                row = slice(f * B, f * B + B)
                here = slice(x * ROWS + f * B, x * ROWS + f * B + B)
                new = rest_ref[pair, row, cols] + total_ref[pair, row, cols]
                new_ref[here, :] = new
                mid_ref[x * PITCH + f * B : x * PITCH + f * B + B, :] = 0.5 * (coarse_ref[here, :] + new)

    lane8 = lanes_of((8, 128))
    within = lane8 % 32
    base = jnp.where(within < 16, within % 8, jnp.where(within < 24, -1, 8))
    window = lane8 % 8

    def box(w, _):
        member, ox, oy, oz = box_place(owner_ref, offset_ref, w)
        z0 = w * B + oz
        pick = base + z0
        pick_x = window + z0
        corner = ox * PITCH + oy - 1
        for f in range(F):
            acc = jnp.zeros((8, 128), F32)
            for t, ref in enumerate((old_ref, mid_ref)):
                for y in range(H + 2):
                    rows = ref[pl.ds(corner + f * B + y, H, stride=PITCH), :]
                    moved = jnp.take_along_axis(rows, pick, axis=1, mode="promise_in_bounds")
                    if y == 0:
                        put = (lane8 >= 32 * t) & (lane8 < 32 * t + 8)
                    elif y == H + 1:
                        put = (lane8 >= 32 * t + 8) & (lane8 < 32 * t + 16)
                    else:
                        put = (lane8 == 32 * t + 15 + y) | (lane8 == 32 * t + 23 + y)
                    acc = jnp.where(put, moved, acc)
            out_ref[member, f * 8 : f * 8 + 8, :] = acc
        for t, ref in enumerate((old_ref, mid_ref)):
            for side, x in enumerate((ox - 1, ox + H)):
                first = jnp.zeros((8, 128), F32)
                second = jnp.zeros((8, 128), F32)
                for y in range(H):
                    put = (lane8 >= 64 + y * 8) & (lane8 < 72 + y * 8)
                    at = x * PITCH + oy + y
                    rows = ref[pl.ds(at, 8, stride=B), :]
                    first = jnp.where(put, jnp.take_along_axis(rows, pick_x, axis=1, mode="promise_in_bounds"), first)
                    tail = jnp.concatenate(
                        [ref[pl.ds(at + 8 * B, F - 8, stride=B), :], jnp.zeros((16 - F, 128), F32)], axis=0
                    )
                    second = jnp.where(
                        put, jnp.take_along_axis(tail, pick_x, axis=1, mode="promise_in_bounds"), second
                    )
                at = (2 * t + side) * 16
                old = out_ref[member, at : at + 16, :]
                out_ref[member, at : at + 16, :] = jnp.where(
                    lanes_of((16, 128)) < 64, old, jnp.concatenate([first, second], axis=0)
                )
        return 0

    lax.fori_loop(0, BOXES, box, 0, unroll=2)


def fine_kernel(
    owner_ref, fine_ref, arrived_ref, coef_ref, const_ref, out_ref, back_ref, hi_ref, lo_ref, wide_ref, rest_ref, total_ref, value_ref, face_out_ref, parts_ref, mixed_ref, back_scratch, source_ref
):
    for slot in range(FSLOTS):
        source_ref[slot] = -1
    device = device_index()
    line = lax.axis_index("gz")
    for member in range(GROUP):
        for w in range(BOXES):
            holder = owner_ref[(member * LINES + line) * BOXES + w]
            source_ref[jnp.where(holder // FSLOTS == device, holder % FSLOTS, FSLOTS)] = member
    held = sum(jnp.where(source_ref[slot] >= 0, 1, 0) for slot in range(FSLOTS))
    batches = (held + BATCH - 1) // BATCH
    constant = {name: const_ref.at[at] for name, at in CONST.items()}

    def batch(i, _):
        first_slot = i * BATCH
        sources = [source_ref[first_slot + k] for k in range(BATCH)]
        lane = lanes_of((B, 128))
        column = lane % B
        for k in range(BATCH):
            message = arrived_ref.at[jnp.maximum(sources[k], 0)]
            for at in range(0, HALF, 16):
                value = message[at : at + 16, :]
                hi, lo = split(value)
                parts_ref[k, at : at + 16, :] = hi
                parts_ref[k, HALF + at : HALF + at + 16, :] = lo
                if at < 64:
                    hi = hi.astype(F32)
                    mixed_ref[k, ROWS + at : ROWS + at + 16, :] = jnp.where(
                        lane < 64, pltpu.roll(value - hi, 64, 1), hi
                    ).astype(BF16)
        for k in range(BATCH):
            lifted = dot(constant["up"][...], parts_ref[k])
            for f in range(F):
                value = lifted[f * B : f * B + B]
                hi = value.astype(BF16).astype(F32)
                mixed_ref[k, f * B : f * B + B, :] = jnp.where(lane < 64, hi, pltpu.roll(value - hi, 64, 1)).astype(
                    BF16
                )
        for k in range(BATCH):
            wide_ref[k] = dot(mixed_ref[k, 0:ROWS, :], constant["ghost"][...])
            face_out_ref[k] = dot(mixed_ref[k, ROWS : ROWS + 64, :], constant["face"][...])
        for t in range(2):
            at = 384 * t
            for k in range(BATCH):
                for f in range(F):
                    row = slice(f * B, f * B + B)
                    if t == 0:
                        a, b = fine_ref[first_slot + k, f, :, 0:128], fine_ref[first_slot + k, f, :, 128:256]
                    else:
                        a, b = value_ref[k, row, 0:128], value_ref[k, row, 128:256]
                    gy = wide_ref[k, row, at : at + 128]
                    gz_a = wide_ref[k, row, at + 128 : at + 256]
                    gz_b = wide_ref[k, row, at + 256 : at + 384]
                    a_up, b_up = pltpu.roll(a, 112, 1), pltpu.roll(b, 112, 1)
                    a_down, b_down = pltpu.roll(a, 16, 1), pltpu.roll(b, 16, 1)
                    yp = (jnp.where(lane < 112, a_up, b_up), jnp.where(lane < 112, b_up, gy))
                    ym = (jnp.where(lane < 16, gy, a_down), jnp.where(lane < 16, a_down, b_down))
                    zp = (
                        jnp.where(column == B - 1, gz_a, pltpu.roll(a, 127, 1)),
                        jnp.where(column == B - 1, gz_b, pltpu.roll(b, 127, 1)),
                    )
                    zm = (
                        jnp.where(column == 0, gz_a, pltpu.roll(a, 1, 1)),
                        jnp.where(column == 0, gz_b, pltpu.roll(b, 1, 1)),
                    )
                    for h, v in enumerate((a, b)):
                        cols = slice(128 * h, 128 * h + 128)
                        put_parts(
                            hi_ref.at[k],
                            lo_ref.at[k],
                            cols,
                            ((f * B, v), (ROWS + f * B, yp[h] - ym[h]), (2 * ROWS + f * B, zp[h] - zm[h])),
                        )
                        rest_ref[k, row, cols] = 0.25 * v + 0.125 * ((yp[h] + ym[h]) + (zp[h] + zm[h]))
                put_parts(
                    hi_ref.at[k], lo_ref.at[k], slice(None), ((3 * ROWS, face_out_ref[k, 32 * t : 32 * t + 32, :]),)
                )
            for k in range(BATCH):
                product(coef_ref, hi_ref.at[k], lo_ref.at[k], total_ref.at[k])
            for k in range(BATCH):
                for f in range(F):
                    row = slice(f * B, f * B + B)
                    value = rest_ref[k, row, :] + total_ref[k, row, :]
                    if t == 0:
                        value_ref[k, row, :] = value
                    else:
                        out_ref[first_slot + k, f] = jnp.where(sources[k] >= 0, value, 0.0)
                        hi, lo = split(value)
                        hi_ref[k, row, :] = hi
                        hi_ref[k, ROWS + f * B : ROWS + f * B + B, :] = lo
        for k in range(BATCH):
            paired = dot(constant["pair"][...], hi_ref[k, 0 : 2 * ROWS, :])
            hi, lo = split(paired)
            means = dot(hi, constant["mean"][...]) + dot(lo, constant["mean"][...])
            back_scratch[k] = jnp.where(
                lanes_of((HALF // 2, 128)) < 64, means[: HALF // 2], pltpu.roll(means[HALF // 2 :], 64, 1)
            )

        for k in range(BATCH):

            @pl.when(sources[k] >= 0)
            def _():
                back_ref[sources[k]] = back_scratch[k]

        return 0

    lax.fori_loop(0, batches, batch, 0)

    def empty(i, _):
        for k in range(BATCH):
            out_ref[i * BATCH + k] = jnp.zeros(out_ref.shape[1:], F32)
        return 0

    lax.fori_loop(batches, FSLOTS // BATCH, empty, 0)


def place_kernel(owner_ref, offset_ref, new_ref, back_ref, out_ref, work_ref, sems):
    for x in range(B):
        work_ref[x * PITCH : x * PITCH + ROWS, :] = new_ref[x * ROWS : (x + 1) * ROWS, :]
    lane = lanes_of((8, 128))

    def box(w, _):
        member, ox, oy, oz = box_place(owner_ref, offset_ref, w)
        z0 = w * B + oz
        inside = (lane >= z0) & (lane < z0 + H)
        pick = jnp.where(inside, lane - z0, 0)
        corner = ox * PITCH + oy
        for f in range(F):
            tile = back_ref[member, f % 5 * 8 : f % 5 * 8 + 8, :]
            rows = [pl.ds(corner + f * B + y, H, stride=PITCH) for y in range(H)]
            before = [work_ref[r, :] for r in rows]
            for y in range(H):
                moved = jnp.take_along_axis(tile, pick + (f // 5 * 64 + y * 8), axis=1, mode="promise_in_bounds")
                work_ref[rows[y], :] = jnp.where(inside, moved, before[y])
        return 0

    lax.fori_loop(0, BOXES, box, 0)
    copies = [
        pltpu.make_async_copy(
            work_ref.at[x * PITCH : x * PITCH + ROWS, :], out_ref.at[x * ROWS : (x + 1) * ROWS, :], sems.at[x]
        )
        for x in range(B)
    ]
    for copy in copies:
        copy.start()
    for copy in copies:
        copy.wait()


def call(kernel, operands, outs, limit, scratch=(), out_space=pltpu.VMEM):
    spaces = [pltpu.SMEM if a.dtype == jnp.int32 else pltpu.VMEM for a in operands]
    return pl.pallas_call(
        kernel,
        in_specs=[pl.BlockSpec(memory_space=space) for space in spaces],
        out_specs=[pl.BlockSpec(memory_space=out_space) for _ in outs],
        out_shape=[jax.ShapeDtypeStruct(*out) for out in outs],
        scratch_shapes=list(scratch),
        compiler_params=pltpu.CompilerParams(vmem_limit_bytes=limit * MIB),
    )(*operands)


def local(coarse_state, fine_state, flux_jacobians, fine_owner, fine_offset):
    rows = coarse_state.reshape(B * ROWS, 128)
    fine_rows = jnp.transpose(fine_state, (0, 2, 1, 3))
    offset = jnp.transpose(fine_offset, (1, 0))
    jacobians = jnp.transpose(flux_jacobians, (1, 0, 2))

    face = ((ROWS, 128), F32)
    x_first, x_last, y_first, y_last, z_first, z_last = call(faces_kernel, (rows,), [face] * 6, 4)

    def from_below(value, axis):
        n = lax.axis_size(axis)
        return lax.ppermute(value, axis, [(i, (i + 1) % n) for i in range(n)])

    def from_above(value, axis):
        n = lax.axis_size(axis)
        return lax.ppermute(value, axis, [((i + 1) % n, i) for i in range(n)])

    halo = (
        from_below(x_last, "gx"),
        from_above(x_first, "gx"),
        from_below(y_last, "gy"),
        from_above(y_first, "gy"),
        from_below(z_last, "gz"),
        from_above(z_first, "gz"),
    )
    new, outgoing, coef = call(
        coarse_kernel,
        (fine_owner, offset, rows, *halo, jacobians),
        [((B * ROWS, 128), F32), ((GROUP, HALF, 128), F32), ((2, ROWS, 512), BF16)],
        14,
        [pltpu.VMEM((B * PITCH, 128), F32)] * 2
        + [pltpu.VMEM((B // 2, 512, 256), BF16)] * 2
        + [pltpu.VMEM((B // 2, ROWS, 256), F32)] * 2
        + [pltpu.VMEM((2, ROWS, 512), BF16), pltpu.VMEM((3, 16, 128), F32)],
    )
    arrived = lax.all_to_all(outgoing, ("gx", "gy"), split_axis=0, concat_axis=0, tiled=True)

    fine_new, returning = call(
        fine_kernel,
        (fine_owner, fine_rows, arrived, coef, fine_constants()),
        [((FSLOTS, F, B, 256), F32), ((GROUP, HALF // 2, 128), F32)],
        20,
        [pltpu.VMEM((BATCH, 512, 256), BF16)] * 2
        + [pltpu.VMEM((BATCH, ROWS, 768), F32)]
        + [pltpu.VMEM((BATCH, ROWS, 256), F32)] * 3
        + [
            pltpu.VMEM((BATCH, 64, 256), F32),
            pltpu.VMEM((BATCH, 2 * HALF, 128), BF16),
            pltpu.VMEM((BATCH, ROWS + 64, 128), BF16),
            pltpu.VMEM((BATCH, HALF // 2, 128), F32),
            pltpu.SMEM((FSLOTS + 1,), jnp.int32),
        ],
    )
    came_back = lax.all_to_all(returning, ("gx", "gy"), split_axis=0, concat_axis=0, tiled=True)

    coarse_out = call(
        place_kernel,
        (fine_owner, offset, new, came_back),
        [((B * ROWS, 128), F32)],
        4,
        [pltpu.VMEM((B * PITCH, 128), F32), pltpu.SemaphoreType.DMA((B,))],
        pl.ANY,
    )[0]
    return coarse_out.reshape(coarse_state.shape), jnp.transpose(fine_new, (0, 2, 1, 3))


def solution(mesh):
    in_specs = (P("gx", None, "gy", "gz"), P(("gx", "gy", "gz"), None, None, None), P(), P(), P())
    out_specs = (P("gx", None, "gy", "gz"), P(("gx", "gy", "gz"), None, None, None))
    return jax.shard_map(local, mesh=mesh, in_specs=in_specs, out_specs=out_specs, check_vma=False)
```

```python
import functools

import jax
import jax.numpy as jnp
import ml_dtypes
import numpy as np
from jax import lax
from jax.experimental import pallas as pl
from jax.experimental.pallas import tpu as pltpu
from jax.sharding import PartitionSpec as P

F = 10
B = 16
BOXES = 8
H = 8
FSLOTS = 16
LINES = 8
GROUP = 16
ROWS = F * B
HALF = F * H
F32 = jnp.float32
BF16 = jnp.bfloat16
MIB = 1024 * 1024
PITCH = ROWS + 8
BATCH = 8


def dot(a, b):
    return jnp.dot(a, b, preferred_element_type=F32)


def split(v):
    hi = v.astype(BF16)
    return hi, (v - hi.astype(F32)).astype(BF16)


def lanes_of(shape):
    return lax.broadcasted_iota(jnp.int32, shape, len(shape) - 1)


CONST = {
    "ghost": (slice(0, 128), slice(0, 768)),
    "face": (slice(0, 128), slice(768, 1024)),
    "mean": (slice(0, 256), slice(1024, 1152)),
}


def fine_constants():
    ghost = np.zeros((128, 768), np.float32)
    face = np.zeros((128, 256), np.float32)
    mean = np.zeros((256, 128), np.float32)
    for part in range(2):
        for t in range(2):
            for j in range(B):
                low, col = part * 64 + t * 32 + j // 2, t * 384
                ghost[low, col + j] = 1
                ghost[low + 8, col + 112 + j] = 1
                ghost[low + 16, col + 128 + j * B] = 1
                ghost[low + 24, col + 128 + j * B + B - 1] = 1
        for y in range(B):
            for z in range(B):
                face[part * 64 + y // 2 * H + z // 2, y * B + z] = 1
                mean[y * B + z, y // 2 * H + z // 2] = 0.125
    every = np.zeros((256, 1152), np.float32)
    for name, value in (("ghost", ghost), ("face", face), ("mean", mean)):
        rows, cols = CONST[name]
        every[rows, cols] = value
    return every.astype(ml_dtypes.bfloat16)


def device_index():
    return (lax.axis_index("gx") * lax.axis_size("gy") + lax.axis_index("gy")) * lax.axis_size("gz") + lax.axis_index("gz")


def box_place(owner_ref, offset_ref, w):
    box = device_index() * BOXES + w
    return (lax.shift_right_logical(owner_ref[box], 7), *(offset_ref[d, box] for d in range(3)))


def fetch(src, dst, sem):
    copy = pltpu.make_async_copy(src, dst, sem)
    copy.start()
    return copy


def coefficients(jac_ref, pad_ref, outs):
    pad_ref[...] = jnp.zeros(pad_ref.shape, F32)
    for d in range(3):
        for g in range(F):
            pad_ref[d, g : g + 1, 0:F] = jac_ref[g, d : d + 1, :]
    row, lane = (lax.broadcasted_iota(jnp.int32, (128, 128), d) for d in range(2))
    eye = jnp.where((row[:16] == lane[:16]) & (row[:16] < F), 0.125, 0.0).astype(F32)
    scaled = [0.125 * pad_ref[d] for d in range(3)]
    row, col = (lax.broadcasted_iota(jnp.int32, (128, 512), d) for d in range(2))
    block, inner = col // ROWS, col % ROWS // B
    ghost = 3 * ROWS
    target = jnp.where(col < ghost, inner + jnp.where(block == 0, 0, 16 + 16 * block), (col + 16) % 32)
    one = lambda cond: jnp.where(cond, 1.0, 0.0).astype(F32)
    first = one(row == target).astype(BF16)
    second = one((col < ROWS) & (row == 16 + inner)).astype(BF16)
    row, col = (lax.broadcasted_iota(jnp.int32, (ROWS, 512), d) for d in range(2))
    here, there = row % B, col % B
    edge = jnp.where(col < ghost + 16, 0, B - 1)
    distance = jnp.where(col < ROWS, there - here - 1, jnp.where(col < ghost, there - here, here - edge))
    mask_first = one(distance == 0)
    mask_second = one((col < ROWS) & (there + 1 == here))
    row, col = (lax.broadcasted_iota(jnp.int32, (ROWS, 128), d) for d in range(2))
    rows = one(row // B == col).astype(BF16)
    pad = jnp.zeros((112, 512), BF16)
    for (s, a, b), out in zip(((1, 0, 2), (0, 1, 2)), outs):
        coef = (
            (eye - scaled[s])
            + pltpu.roll(eye + scaled[s], 16, 1)
            - pltpu.roll(scaled[a], 32, 1)
            - pltpu.roll(scaled[b], 48, 1)
        )
        for part, value in enumerate(split(coef)):
            wide1 = jnp.concatenate([dot(value, first).astype(BF16), pad], axis=0)
            wide2 = jnp.concatenate([dot(value, second).astype(BF16), pad], axis=0)
            out[part] = (dot(rows, wide1) * mask_first + dot(rows, wide2) * mask_second).astype(BF16)


def faces_kernel(coarse_ref, x_lo, x_hi, y_lo, y_hi, z_lo, z_hi):
    x_lo[...] = coarse_ref[0:ROWS, :]
    x_hi[...] = coarse_ref[(B - 1) * ROWS : B * ROWS, :]
    for x in range(B):
        y_lo[x * F : x * F + F, :] = coarse_ref[pl.ds(x * ROWS, F, stride=B), :]
        y_hi[x * F : x * F + F, :] = coarse_ref[pl.ds(x * ROWS + B - 1, F, stride=B), :]
    lane = lanes_of((ROWS, 128))
    low = jnp.zeros((ROWS, 128), F32)
    high = jnp.zeros((ROWS, 128), F32)
    for x in range(B):
        plane = coarse_ref[x * ROWS : (x + 1) * ROWS, :]
        low = jnp.where(lane == x, pltpu.roll(plane, x, 1), low)
        high = jnp.where(lane == x, pltpu.roll(plane, x + 1, 1), high)
    z_lo[...] = low
    z_hi[...] = high


def product(coef_ref, hi_ref, lo_ref, total_ref):
    both = dot(coef_ref[...].reshape(2 * ROWS, 512), hi_ref[...])
    total_ref[...] = both[:ROWS] + both[ROWS:] + dot(coef_ref[0], lo_ref[...])


def put_parts(hi_ref, lo_ref, cols, parts):
    for at, value in parts:
        hi, lo = split(value)
        hi_ref[at : at + value.shape[0], cols] = hi
        lo_ref[at : at + value.shape[0], cols] = lo


def coarse_kernel(
    owner_hbm, offset_hbm, coarse_ref, x_lo, x_hi, y_lo, y_hi, z_lo, z_hi, jac_hbm, new_ref, out_ref, fine_coef_ref, old_ref,
    mid_ref, hi_ref, lo_ref, rest_ref, total_ref, coef_ref, pad_ref,
    owner_ref, offset_ref, jac_ref, sems
):
    fetch_owner = fetch(owner_hbm, owner_ref, sems.at[0])
    fetch_offset = fetch(offset_hbm, offset_ref, sems.at[1])
    fetch(jac_hbm, jac_ref, sems.at[2]).wait()
    coefficients(jac_ref, pad_ref, (coef_ref, fine_coef_ref))
    lane = lanes_of((B, 128))
    ghost_zero = jnp.zeros((16 - F, 128), F32)
    for pair in range(B // 2):
        for side in range(2):
            x = 2 * pair + side
            cols = slice(side * 128, side * 128 + 128)
            for f in range(F):
                row = slice(f * B, f * B + B)
                here = x * ROWS + f * B
                p = coarse_ref[here : here + B, :]
                xm = coarse_ref[here - ROWS : here - ROWS + B, :] if x > 0 else x_lo[row, :]
                xp = coarse_ref[here + ROWS : here + ROWS + B, :] if x < B - 1 else x_hi[row, :]
                zm = jnp.where(lane == 0, pltpu.roll(z_lo[row, :], (128 - x) % 128, 1), pltpu.roll(p, 1, 1))
                zp = jnp.where(lane == 127, pltpu.roll(z_hi[row, :], 127 - x, 1), pltpu.roll(p, 127, 1))
                put_parts(
                    hi_ref.at[pair],
                    lo_ref.at[pair],
                    cols,
                    ((f * B, p), (ROWS + f * B, xp - xm), (2 * ROWS + f * B, zp - zm)),
                )
                rest_ref[pair, row, cols] = 0.25 * p + 0.125 * ((xp + xm) + (zp + zm))
                old_ref[x * PITCH + f * B : x * PITCH + f * B + B, :] = p
            low = jnp.concatenate([y_lo[x * F : x * F + F, :], ghost_zero], axis=0)
            high = jnp.concatenate([y_hi[x * F : x * F + F, :], ghost_zero], axis=0)
            put_parts(hi_ref.at[pair], lo_ref.at[pair], cols, ((3 * ROWS, low), (3 * ROWS + 16, high)))
    for pair in range(B // 2):
        product(coef_ref, hi_ref.at[pair], lo_ref.at[pair], total_ref.at[pair])
    for pair in range(B // 2):
        for side in range(2):
            x = 2 * pair + side
            cols = slice(side * 128, side * 128 + 128)
            for f in range(F):
                row = slice(f * B, f * B + B)
                here = slice(x * ROWS + f * B, x * ROWS + f * B + B)
                new = rest_ref[pair, row, cols] + total_ref[pair, row, cols]
                new_ref[here, :] = new
                mid_ref[x * PITCH + f * B : x * PITCH + f * B + B, :] = 0.5 * (coarse_ref[here, :] + new)

    fetch_owner.wait()
    fetch_offset.wait()
    lane8 = lanes_of((8, 128))
    within = lane8 % 32
    base = jnp.where(within < 16, within % 8, jnp.where(within < 24, -1, 8))
    window = lane8 % 8

    def box(w, _):
        member, ox, oy, oz = box_place(owner_ref, offset_ref, w)
        z0 = w * B + oz
        pick = base + z0
        pick_x = window + z0
        corner = ox * PITCH + oy - 1
        for f in range(F):
            acc = jnp.zeros((8, 128), F32)
            for t, ref in enumerate((old_ref, mid_ref)):
                for y in range(H + 2):
                    rows = ref[pl.ds(corner + f * B + y, H, stride=PITCH), :]
                    moved = jnp.take_along_axis(rows, pick, axis=1, mode="promise_in_bounds")
                    if y == 0:
                        put = (lane8 >= 32 * t) & (lane8 < 32 * t + 8)
                    elif y == H + 1:
                        put = (lane8 >= 32 * t + 8) & (lane8 < 32 * t + 16)
                    else:
                        put = (lane8 == 32 * t + 15 + y) | (lane8 == 32 * t + 23 + y)
                    acc = jnp.where(put, moved, acc)
            out_ref[member, f * 8 : f * 8 + 8, :] = acc
        for t, ref in enumerate((old_ref, mid_ref)):
            for side, x in enumerate((ox - 1, ox + H)):
                first = jnp.zeros((8, 128), F32)
                second = jnp.zeros((8, 128), F32)
                for y in range(H):
                    put = (lane8 >= 64 + y * 8) & (lane8 < 72 + y * 8)
                    at = x * PITCH + oy + y
                    rows = ref[pl.ds(at, 8, stride=B), :]
                    first = jnp.where(put, jnp.take_along_axis(rows, pick_x, axis=1, mode="promise_in_bounds"), first)
                    tail = jnp.concatenate(
                        [ref[pl.ds(at + 8 * B, F - 8, stride=B), :], jnp.zeros((16 - F, 128), F32)], axis=0
                    )
                    second = jnp.where(
                        put, jnp.take_along_axis(tail, pick_x, axis=1, mode="promise_in_bounds"), second
                    )
                at = (2 * t + side) * 16
                old = out_ref[member, at : at + 16, :]
                out_ref[member, at : at + 16, :] = jnp.where(
                    lanes_of((16, 128)) < 64, old, jnp.concatenate([first, second], axis=0)
                )
        return 0

    lax.fori_loop(0, BOXES, box, 0, unroll=2)


def fine_kernel(
    owner_hbm, fine_hbm, arrived_ref, coef_ref, const_ref, out_hbm, back_ref, hi_ref, lo_ref, wide_ref, rest_ref,
    total_ref, value_ref, face_out_ref, spread_ref, mixed_ref, mean_ref, source_ref, owner_ref, fine_ref, out_ref, sems
):
    fetch_owner = fetch(owner_hbm, owner_ref, sems.at[0])
    batches_at = [slice(i * BATCH, i * BATCH + BATCH) for i in range(FSLOTS // BATCH)]
    fetch_fine = [fetch(fine_hbm.at[at], fine_ref.at[at], sems.at[1 + i]) for i, at in enumerate(batches_at)]
    for slot in range(FSLOTS):
        source_ref[slot] = -1
    first_here = device_index() * FSLOTS
    line = lax.axis_index("gz")
    fetch_owner.wait()
    for member in range(GROUP):
        for w in range(BOXES):
            holder = owner_ref[(member * LINES + line) * BOXES + w]
            source_ref[jnp.minimum(holder ^ first_here, FSLOTS)] = member
    held = sum(jnp.where(source_ref[slot] >= 0, 1, 0) for slot in range(FSLOTS))
    batches = (held + BATCH - 1) // BATCH
    constant = {name: const_ref.at[at] for name, at in CONST.items()}
    for copy in fetch_fine:
        copy.wait()

    def write_out(i):
        at = pl.ds(i * BATCH, BATCH)
        return pltpu.make_async_copy(out_ref.at[at], out_hbm.at[at], sems.at[3 + i])

    def batch(i, _):
        first_slot = i * BATCH
        sources = [source_ref[first_slot + k] for k in range(BATCH)]
        lane = lanes_of((B, 128))
        column = lane % B
        lane8 = lanes_of((8, 128))
        for k in range(BATCH):
            message = arrived_ref.at[jnp.maximum(sources[k], 0)]
            for at in range(0, 64, 16):
                value = message[at : at + 16, :]
                hi = value.astype(BF16).astype(F32)
                mixed_ref[k, ROWS + at : ROWS + at + 16, :] = jnp.where(
                    lane < 64, pltpu.roll(value - hi, 64, 1), hi
                ).astype(BF16)
            for f in range(F):
                value = message[f * H : f * H + H, :]
                hi = value.astype(BF16).astype(F32)
                both = jnp.where(lane8 < 64, hi, pltpu.roll(value - hi, 64, 1))
                spread_ref[k, pl.ds(f * B, H, stride=2), :] = both
                spread_ref[k, pl.ds(f * B + 1, H, stride=2), :] = both
        for k in range(BATCH):
            for f in range(F):
                row = slice(f * B, f * B + B)
                mixed_ref[k, row, :] = spread_ref[k, row, :].astype(BF16)
        for k in range(BATCH):
            wide_ref[k] = dot(mixed_ref[k, 0:ROWS, :], constant["ghost"][...])
            face_out_ref[k] = dot(mixed_ref[k, ROWS : ROWS + 64, :], constant["face"][...])
        for t in range(2):
            at = 384 * t
            for k in range(BATCH):
                for f in range(F):
                    row = slice(f * B, f * B + B)
                    if t == 0:
                        a, b = fine_ref[first_slot + k, f, :, 0:128], fine_ref[first_slot + k, f, :, 128:256]
                    else:
                        a, b = value_ref[k, row, 0:128], value_ref[k, row, 128:256]
                    gy = wide_ref[k, row, at : at + 128]
                    gz_a = wide_ref[k, row, at + 128 : at + 256]
                    gz_b = wide_ref[k, row, at + 256 : at + 384]
                    a_up, b_up = pltpu.roll(a, 112, 1), pltpu.roll(b, 112, 1)
                    a_down, b_down = pltpu.roll(a, 16, 1), pltpu.roll(b, 16, 1)
                    yp = (jnp.where(lane < 112, a_up, b_up), jnp.where(lane < 112, b_up, gy))
                    ym = (jnp.where(lane < 16, gy, a_down), jnp.where(lane < 16, a_down, b_down))
                    zp = (
                        jnp.where(column == B - 1, gz_a, pltpu.roll(a, 127, 1)),
                        jnp.where(column == B - 1, gz_b, pltpu.roll(b, 127, 1)),
                    )
                    zm = (
                        jnp.where(column == 0, gz_a, pltpu.roll(a, 1, 1)),
                        jnp.where(column == 0, gz_b, pltpu.roll(b, 1, 1)),
                    )
                    for h, v in enumerate((a, b)):
                        cols = slice(128 * h, 128 * h + 128)
                        put_parts(
                            hi_ref.at[k],
                            lo_ref.at[k],
                            cols,
                            ((f * B, v), (ROWS + f * B, yp[h] - ym[h]), (2 * ROWS + f * B, zp[h] - zm[h])),
                        )
                        rest_ref[k, row, cols] = 0.25 * v + 0.125 * ((yp[h] + ym[h]) + (zp[h] + zm[h]))
                put_parts(
                    hi_ref.at[k], lo_ref.at[k], slice(None), ((3 * ROWS, face_out_ref[k, 32 * t : 32 * t + 32, :]),)
                )
            for k in range(BATCH):
                product(coef_ref, hi_ref.at[k], lo_ref.at[k], total_ref.at[k])
            for k in range(BATCH):
                for f in range(F):
                    row = slice(f * B, f * B + B)
                    value = rest_ref[k, row, :] + total_ref[k, row, :]
                    if t == 0:
                        value_ref[k, row, :] = value
                    else:
                        out_ref[first_slot + k, f] = jnp.where(sources[k] >= 0, value, 0.0)
                        hi, lo = split(value)
                        hi_ref[k, row, :] = hi
                        hi_ref[k, ROWS + f * B : ROWS + f * B + B, :] = lo
        write_out(i).start()
        for k in range(BATCH):
            mean_ref[k] = dot(hi_ref[k, 0:ROWS, :], constant["mean"][...]) + dot(
                hi_ref[k, ROWS : 2 * ROWS, :], constant["mean"][...]
            )
        for k in range(BATCH):

            @pl.when(sources[k] >= 0)
            def _():
                for f in range(F // 2):
                    halves = [
                        mean_ref[k, pl.ds(g * B, H, stride=2), :] + mean_ref[k, pl.ds(g * B + 1, H, stride=2), :]
                        for g in (f, f + F // 2)
                    ]
                    back_ref[sources[k], f * H : f * H + H, :] = jnp.where(
                        lane8 < 64, halves[0], pltpu.roll(halves[1], 64, 1)
                    )

        return 0

    lax.fori_loop(0, batches, batch, 0)

    def empty(i, _):
        for k in range(BATCH):
            out_ref[i * BATCH + k] = jnp.zeros(out_ref.shape[1:], F32)
        write_out(i).start()
        return 0

    lax.fori_loop(batches, FSLOTS // BATCH, empty, 0)
    for i in range(FSLOTS // BATCH):
        write_out(i).wait()


def place_kernel(owner_hbm, offset_hbm, new_ref, back_ref, out_ref, work_ref, sems, owner_ref, offset_ref):
    fetch_owner = fetch(owner_hbm, owner_ref, sems.at[B])
    fetch_offset = fetch(offset_hbm, offset_ref, sems.at[B + 1])
    for x in range(B):
        work_ref[x * PITCH : x * PITCH + ROWS, :] = new_ref[x * ROWS : (x + 1) * ROWS, :]
    fetch_owner.wait()
    fetch_offset.wait()
    lane = lanes_of((8, 128))

    def box(w, _):
        member, ox, oy, oz = box_place(owner_ref, offset_ref, w)
        z0 = w * B + oz
        inside = (lane >= z0) & (lane < z0 + H)
        pick = jnp.where(inside, lane - z0, 0)
        corner = ox * PITCH + oy
        for f in range(F):
            tile = back_ref[member, f % 5 * 8 : f % 5 * 8 + 8, :]
            rows = [pl.ds(corner + f * B + y, H, stride=PITCH) for y in range(H)]
            before = [work_ref[r, :] for r in rows]
            for y in range(H):
                moved = jnp.take_along_axis(tile, pick + (f // 5 * 64 + y * 8), axis=1, mode="promise_in_bounds")
                work_ref[rows[y], :] = jnp.where(inside, moved, before[y])
        return 0

    lax.fori_loop(0, BOXES, box, 0)
    copies = [
        pltpu.make_async_copy(
            work_ref.at[x * PITCH : x * PITCH + ROWS, :], out_ref.at[x * ROWS : (x + 1) * ROWS, :], sems.at[x]
        )
        for x in range(B)
    ]
    for copy in copies:
        copy.start()
    for copy in copies:
        copy.wait()


INDEX = [pltpu.SMEM((BOXES * LINES * GROUP,), jnp.int32), pltpu.SMEM((3, BOXES * LINES * GROUP), jnp.int32)]


def call(kernel, operands, outs, limit, scratch=(), hbm=(), hbm_outs=()):
    space = lambda cond: pl.BlockSpec(memory_space=pltpu.HBM if cond else pltpu.VMEM)
    return pl.pallas_call(
        kernel,
        in_specs=[space(i in hbm) for i in range(len(operands))],
        out_specs=[space(i in hbm_outs) for i in range(len(outs))],
        out_shape=[jax.ShapeDtypeStruct(*out) for out in outs],
        scratch_shapes=list(scratch),
        compiler_params=pltpu.CompilerParams(vmem_limit_bytes=limit * MIB),
    )(*operands)


def local(coarse_state, fine_state, flux_jacobians, fine_owner, fine_offset):
    rows = coarse_state.reshape(B * ROWS, 128)
    fine_rows = jnp.transpose(fine_state, (0, 2, 1, 3))
    offset = jnp.transpose(fine_offset, (1, 0))
    jacobians = jnp.transpose(flux_jacobians, (1, 0, 2))

    face = ((ROWS, 128), F32)
    x_first, x_last, y_first, y_last, z_first, z_last = call(faces_kernel, (rows,), [face] * 6, 4)

    def from_below(value, axis):
        n = lax.axis_size(axis)
        return lax.ppermute(value, axis, [(i, (i + 1) % n) for i in range(n)])

    def from_above(value, axis):
        n = lax.axis_size(axis)
        return lax.ppermute(value, axis, [((i + 1) % n, i) for i in range(n)])

    halo = (
        from_below(x_last, "gx"),
        from_above(x_first, "gx"),
        from_below(y_last, "gy"),
        from_above(y_first, "gy"),
        from_below(z_last, "gz"),
        from_above(z_first, "gz"),
    )
    new, outgoing, coef = call(
        coarse_kernel,
        (fine_owner, offset, rows, *halo, jacobians),
        [((B * ROWS, 128), F32), ((GROUP, HALF, 128), F32), ((2, ROWS, 512), BF16)],
        14,
        [pltpu.VMEM((B * PITCH, 128), F32)] * 2
        + [pltpu.VMEM((B // 2, 512, 256), BF16)] * 2
        + [pltpu.VMEM((B // 2, ROWS, 256), F32)] * 2
        + [pltpu.VMEM((2, ROWS, 512), BF16), pltpu.VMEM((3, 16, 128), F32)]
        + INDEX
        + [pltpu.VMEM((F, 3, F), F32), pltpu.SemaphoreType.DMA((3,))],
        hbm=(0, 1, 9),
    )
    arrived = lax.all_to_all(outgoing, ("gx", "gy"), split_axis=0, concat_axis=0, tiled=True)

    fine_new, returning = call(
        fine_kernel,
        (fine_owner, fine_rows, arrived, coef, fine_constants()),
        [((FSLOTS, F, B, 256), F32), ((GROUP, HALF // 2, 128), F32)],
        24,
        [pltpu.VMEM((BATCH, 512, 256), BF16)] * 2
        + [pltpu.VMEM((BATCH, ROWS, 768), F32)]
        + [pltpu.VMEM((BATCH, ROWS, 256), F32)] * 3
        + [
            pltpu.VMEM((BATCH, 64, 256), F32),
            pltpu.VMEM((BATCH, ROWS, 128), F32),
            pltpu.VMEM((BATCH, ROWS + 64, 128), BF16),
            pltpu.VMEM((BATCH, ROWS, 128), F32),
            pltpu.SMEM((FSLOTS + 1,), jnp.int32),
            INDEX[0],
            pltpu.VMEM((FSLOTS, F, B, 256), F32),
            pltpu.VMEM((FSLOTS, F, B, 256), F32),
            pltpu.SemaphoreType.DMA((1 + 2 * (FSLOTS // BATCH),)),
        ],
        hbm=(0, 1),
        hbm_outs=(0,),
    )
    came_back = lax.all_to_all(returning, ("gx", "gy"), split_axis=0, concat_axis=0, tiled=True)

    coarse_out = call(
        place_kernel,
        (fine_owner, offset, new, came_back),
        [((B * ROWS, 128), F32)],
        4,
        [pltpu.VMEM((B * PITCH, 128), F32), pltpu.SemaphoreType.DMA((B + 2,))] + INDEX,
        hbm=(0, 1),
        hbm_outs=(0,),
    )[0]
    return coarse_out.reshape(coarse_state.shape), jnp.transpose(fine_new, (0, 2, 1, 3))


def solution(mesh):
    in_specs = (P("gx", None, "gy", "gz"), P(("gx", "gy", "gz"), None, None, None), P(), P(), P())
    out_specs = (P("gx", None, "gy", "gz"), P(("gx", "gy", "gz"), None, None, None))
    return jax.shard_map(local, mesh=mesh, in_specs=in_specs, out_specs=out_specs, check_vma=False)
```

```python
import functools

import jax
import jax.numpy as jnp
from jax import lax
from jax.experimental import pallas as pl
from jax.experimental.pallas import tpu as pltpu
from jax.sharding import PartitionSpec as P

F = 10
B = 16
BOXES = 8
H = 8
FSLOTS = 16
LINES = 8
GROUP = 16
ROWS = F * B
HALF = F * H
F32 = jnp.float32
BF16 = jnp.bfloat16
MESSAGE = HALF // 2 + 24
MIB = 1024 * 1024
PITCH = ROWS + 8
BATCH = 8


def dot(a, b):
    return jnp.dot(a, b, preferred_element_type=F32)


def split(v):
    hi = v.astype(BF16)
    return hi, (v - hi.astype(F32)).astype(BF16)


def lanes_of(shape):
    return lax.broadcasted_iota(jnp.int32, shape, len(shape) - 1)


def fine_constants(ghost_ref, face_ref, mean_ref):
    def one(cond):
        return jnp.where(cond, 1.0, 0.0).astype(BF16)

    row, col = (lax.broadcasted_iota(jnp.int32, (128, 384), d) for d in range(2))
    cell = col - 128
    y, z = cell // B, cell % B
    target = jnp.where(
        col < 16,
        col // 2,
        jnp.where(
            col < 112,
            -1,
            jnp.where(
                col < 128,
                8 + (col - 112) // 2,
                jnp.where(z == 0, 16 + y // 2, jnp.where(z == B - 1, 24 + y // 2, -1)),
            ),
        ),
    )
    for t in range(2):
        ghost_ref[:, 384 * t : 384 * t + 384] = one(row % 64 == target + jnp.where(target < 0, -64, 32 * t))
    row, col = (lax.broadcasted_iota(jnp.int32, (128, 256), d) for d in range(2))
    face_ref[...] = one(row % 64 == col // B // 2 * H + col % B // 2)
    row, col = (lax.broadcasted_iota(jnp.int32, (256, 128), d) for d in range(2))
    mean_ref[...] = one(col == row // B // 2 * H + row % B // 2) * jnp.asarray(0.125, BF16)


def device_index():
    return (lax.axis_index("gx") * lax.axis_size("gy") + lax.axis_index("gy")) * lax.axis_size("gz") + lax.axis_index("gz")


def box_place(owner_ref, offset_ref, w):
    box = device_index() * BOXES + w
    return (lax.shift_right_logical(owner_ref[box], 7), *(offset_ref[d, box] for d in range(3)))


def fetch(src, dst, sem):
    copy = pltpu.make_async_copy(src, dst, sem)
    copy.start()
    return copy


def coefficients(jac_ref, pad_ref, outs):
    pad_ref[...] = jnp.zeros(pad_ref.shape, F32)
    for d in range(3):
        for g in range(F):
            pad_ref[d, g : g + 1, 0:F] = jac_ref[g, d : d + 1, :]
    row, lane = (lax.broadcasted_iota(jnp.int32, (128, 128), d) for d in range(2))
    eye = jnp.where((row[:16] == lane[:16]) & (row[:16] < F), 0.125, 0.0).astype(F32)
    scaled = [0.125 * pad_ref[d] for d in range(3)]
    row, col = (lax.broadcasted_iota(jnp.int32, (128, 512), d) for d in range(2))
    block, inner = col // ROWS, col % ROWS // B
    ghost = 3 * ROWS
    target = jnp.where(col < ghost, inner + jnp.where(block == 0, 0, 16 + 16 * block), (col + 16) % 32)
    one = lambda cond: jnp.where(cond, 1.0, 0.0).astype(F32)
    first = one(row == target).astype(BF16)
    second = one((col < ROWS) & (row == 16 + inner)).astype(BF16)
    row, col = (lax.broadcasted_iota(jnp.int32, (ROWS, 512), d) for d in range(2))
    here, there = row % B, col % B
    edge = jnp.where(col < ghost + 16, 0, B - 1)
    distance = jnp.where(col < ROWS, there - here - 1, jnp.where(col < ghost, there - here, here - edge))
    mask_first = one(distance == 0)
    mask_second = one((col < ROWS) & (there + 1 == here))
    row, col = (lax.broadcasted_iota(jnp.int32, (ROWS, 128), d) for d in range(2))
    rows = one(row // B == col).astype(BF16)
    pad = jnp.zeros((112, 512), BF16)
    for (s, a, b), out in zip(((1, 0, 2), (0, 1, 2)), outs):
        coef = (
            (eye - scaled[s])
            + pltpu.roll(eye + scaled[s], 16, 1)
            - pltpu.roll(scaled[a], 32, 1)
            - pltpu.roll(scaled[b], 48, 1)
        )
        for part, value in enumerate(split(coef)):
            wide1 = jnp.concatenate([dot(value, first).astype(BF16), pad], axis=0)
            wide2 = jnp.concatenate([dot(value, second).astype(BF16), pad], axis=0)
            out[part] = (dot(rows, wide1) * mask_first + dot(rows, wide2) * mask_second).astype(BF16)


def faces_kernel(coarse_ref, x_lo, x_hi, y_lo, y_hi, z_lo, z_hi):
    x_lo[...] = coarse_ref[0:ROWS, :]
    x_hi[...] = coarse_ref[(B - 1) * ROWS : B * ROWS, :]
    for x in range(B):
        y_lo[x * F : x * F + F, :] = coarse_ref[pl.ds(x * ROWS, F, stride=B), :]
        y_hi[x * F : x * F + F, :] = coarse_ref[pl.ds(x * ROWS + B - 1, F, stride=B), :]
    lane = lanes_of((ROWS, 128))
    low = jnp.zeros((ROWS, 128), F32)
    high = jnp.zeros((ROWS, 128), F32)
    for x in range(B):
        plane = coarse_ref[x * ROWS : (x + 1) * ROWS, :]
        low = jnp.where(lane == x, pltpu.roll(plane, x, 1), low)
        high = jnp.where(lane == x, pltpu.roll(plane, x + 1, 1), high)
    z_lo[...] = low
    z_hi[...] = high


def product(coef_ref, hi_ref, lo_ref, total_ref):
    both = dot(coef_ref[...].reshape(2 * ROWS, 512), hi_ref[...])
    total_ref[...] = both[:ROWS] + both[ROWS:] + dot(coef_ref[0], lo_ref[...])


def put_parts(hi_ref, lo_ref, cols, parts):
    for at, value in parts:
        hi, lo = split(value)
        hi_ref[at : at + value.shape[0], cols] = hi
        lo_ref[at : at + value.shape[0], cols] = lo


def coarse_kernel(
    owner_hbm, offset_hbm, coarse_ref, x_lo, x_hi, y_lo, y_hi, z_lo, z_hi, jac_hbm, new_ref, out_ref, fine_coef_ref, old_ref,
    mid_ref, hi_ref, lo_ref, rest_ref, total_ref, coef_ref, pad_ref,
    owner_ref, offset_ref, jac_ref, sems
):
    fetch_owner = fetch(owner_hbm, owner_ref, sems.at[0])
    fetch_offset = fetch(offset_hbm, offset_ref, sems.at[1])
    fetch(jac_hbm, jac_ref, sems.at[2]).wait()
    coefficients(jac_ref, pad_ref, (coef_ref, fine_coef_ref))
    lane = lanes_of((B, 128))
    ghost_zero = jnp.zeros((16 - F, 128), F32)
    for pair in range(B // 2):
        for side in range(2):
            x = 2 * pair + side
            cols = slice(side * 128, side * 128 + 128)
            for f in range(F):
                row = slice(f * B, f * B + B)
                here = x * ROWS + f * B
                p = coarse_ref[here : here + B, :]
                xm = coarse_ref[here - ROWS : here - ROWS + B, :] if x > 0 else x_lo[row, :]
                xp = coarse_ref[here + ROWS : here + ROWS + B, :] if x < B - 1 else x_hi[row, :]
                zm = jnp.where(lane == 0, pltpu.roll(z_lo[row, :], (128 - x) % 128, 1), pltpu.roll(p, 1, 1))
                zp = jnp.where(lane == 127, pltpu.roll(z_hi[row, :], 127 - x, 1), pltpu.roll(p, 127, 1))
                put_parts(
                    hi_ref.at[pair],
                    lo_ref.at[pair],
                    cols,
                    ((f * B, p), (ROWS + f * B, xp - xm), (2 * ROWS + f * B, zp - zm)),
                )
                rest_ref[pair, row, cols] = 0.25 * p + 0.125 * ((xp + xm) + (zp + zm))
                old_ref[x * PITCH + f * B : x * PITCH + f * B + B, :] = p
            low = jnp.concatenate([y_lo[x * F : x * F + F, :], ghost_zero], axis=0)
            high = jnp.concatenate([y_hi[x * F : x * F + F, :], ghost_zero], axis=0)
            put_parts(hi_ref.at[pair], lo_ref.at[pair], cols, ((3 * ROWS, low), (3 * ROWS + 16, high)))
    for pair in range(B // 2):
        product(coef_ref, hi_ref.at[pair], lo_ref.at[pair], total_ref.at[pair])
    for pair in range(B // 2):
        for side in range(2):
            x = 2 * pair + side
            cols = slice(side * 128, side * 128 + 128)
            for f in range(F):
                row = slice(f * B, f * B + B)
                here = slice(x * ROWS + f * B, x * ROWS + f * B + B)
                new = rest_ref[pair, row, cols] + total_ref[pair, row, cols]
                new_ref[here, :] = new
                mid_ref[x * PITCH + f * B : x * PITCH + f * B + B, :] = 0.5 * (coarse_ref[here, :] + new)

    fetch_owner.wait()
    fetch_offset.wait()
    lane8 = lanes_of((8, 128))
    within = lane8 % 32
    base = jnp.where(within < 16, within % 8, jnp.where(within < 24, -1, 8))
    window = lane8 % 8

    def box(w, _):
        member, ox, oy, oz = box_place(owner_ref, offset_ref, w)
        z0 = w * B + oz
        pick = base + z0
        pick_x = window + z0
        corner = ox * PITCH + oy - 1
        for f in range(F // 2):
            acc = jnp.zeros((8, 128), F32)
            for half in range(2):
                for t, ref in enumerate((old_ref, mid_ref)):
                    low = 64 * half + 32 * t
                    for y in range(H + 2):
                        rows = ref[pl.ds(corner + (f + 5 * half) * B + y, H, stride=PITCH), :]
                        moved = jnp.take_along_axis(rows, pick, axis=1, mode="promise_in_bounds")
                        if y == 0:
                            put = (lane8 >= low) & (lane8 < low + 8)
                        elif y == H + 1:
                            put = (lane8 >= low + 8) & (lane8 < low + 16)
                        else:
                            put = (lane8 == low + 15 + y) | (lane8 == low + 23 + y)
                        acc = jnp.where(put, moved, acc)
            out_ref[member, f * 8 : f * 8 + 8, :] = acc
        tiles = [jnp.zeros((8, 128), F32)] * 3
        for side, x in enumerate((ox - 1, ox + H)):
            for y in range(H):
                low = 64 * side + 8 * y
                put = (lane8 >= low) & (lane8 < low + 8)
                at = x * PITCH + oy + y
                tails = [ref[pl.ds(at + 8 * B, F - 8, stride=B), :] for ref in (old_ref, mid_ref)]
                values = [ref[pl.ds(at, 8, stride=B), :] for ref in (old_ref, mid_ref)]
                values.append(jnp.concatenate(tails + [jnp.zeros((4, 128), F32)], axis=0))
                for n, value in enumerate(values):
                    moved = jnp.take_along_axis(value, pick_x, axis=1, mode="promise_in_bounds")
                    tiles[n] = jnp.where(put, moved, tiles[n])
        for n in range(3):
            out_ref[member, HALF // 2 + 8 * n : HALF // 2 + 8 * n + 8, :] = tiles[n]
        return 0

    lax.fori_loop(0, BOXES, box, 0, unroll=2)


def fine_kernel(
    owner_hbm, fine_hbm, arrived_ref, coef_ref, out_hbm, back_ref, hi_ref, lo_ref, wide_ref, rest_ref,
    total_ref, value_ref, face_out_ref, spread_ref, mixed_ref, mean_ref, source_ref, owner_ref, fine_ref, out_ref,
    ghost_ref, face_ref, pair_ref, sems
):
    fetch_owner = fetch(owner_hbm, owner_ref, sems.at[0])
    batches_at = [slice(i * BATCH, i * BATCH + BATCH) for i in range(FSLOTS // BATCH)]
    fetch_fine = [fetch(fine_hbm.at[at], fine_ref.at[at], sems.at[1 + i]) for i, at in enumerate(batches_at)]
    for slot in range(FSLOTS):
        source_ref[slot] = -1
    first_here = device_index() * FSLOTS
    line = lax.axis_index("gz")
    fetch_owner.wait()
    for member in range(GROUP):
        for w in range(BOXES):
            holder = owner_ref[(member * LINES + line) * BOXES + w]
            source_ref[jnp.minimum(holder ^ first_here, FSLOTS)] = member
    held = sum(jnp.where(source_ref[slot] >= 0, 1, 0) for slot in range(FSLOTS))
    batches = (held + BATCH - 1) // BATCH
    fine_constants(ghost_ref, face_ref, pair_ref)
    for copy in fetch_fine:
        copy.wait()

    def write_out(i):
        at = pl.ds(i * BATCH, BATCH)
        return pltpu.make_async_copy(out_ref.at[at], out_hbm.at[at], sems.at[3 + i])

    def batch(i, _):
        first_slot = i * BATCH
        sources = [source_ref[first_slot + k] for k in range(BATCH)]
        lane = lanes_of((B, 128))
        column = lane % B
        lane8 = lanes_of((8, 128))
        for k in range(BATCH):
            message = arrived_ref.at[jnp.maximum(sources[k], 0)]
            tail = message[MESSAGE - 8 : MESSAGE, :]
            for t in range(2):
                at = HALF // 2 + 8 * t
                value = jnp.concatenate([message[at : at + 8, :], pltpu.roll(tail, 6, 0) if t else tail], axis=0)
                hi = value.astype(BF16).astype(F32)
                lo = pltpu.roll(value - hi, 64, 1)
                at = ROWS + 32 * t
                mixed_ref[k, at : at + 16, :] = jnp.where(lane < 64, hi, lo).astype(BF16)
                mixed_ref[k, at + 16 : at + 32, :] = jnp.where(lane < 64, lo, hi).astype(BF16)
            for f in range(F):
                value = message[f % 5 * H : f % 5 * H + H, :]
                hi = value.astype(BF16).astype(F32)
                lo = pltpu.roll(value - hi, 64, 1)
                both = jnp.where(lane8 < 64, hi, lo) if f < 5 else jnp.where(lane8 < 64, lo, hi)
                spread_ref[k, pl.ds(f * B, H, stride=2), :] = both
                spread_ref[k, pl.ds(f * B + 1, H, stride=2), :] = both
        for k in range(BATCH):
            for f in range(F):
                row = slice(f * B, f * B + B)
                mixed_ref[k, row, :] = spread_ref[k, row, :].astype(BF16)
        for k in range(BATCH):
            wide_ref[k] = dot(mixed_ref[k, 0:ROWS, :], ghost_ref[...])
            face_out_ref[k] = dot(mixed_ref[k, ROWS : ROWS + 64, :], face_ref[...])
        for t in range(2):
            at = 384 * t
            for k in range(BATCH):
                for f in range(F):
                    row = slice(f * B, f * B + B)
                    if t == 0:
                        a, b = fine_ref[first_slot + k, f, :, 0:128], fine_ref[first_slot + k, f, :, 128:256]
                    else:
                        a, b = value_ref[k, row, 0:128], value_ref[k, row, 128:256]
                    gy = wide_ref[k, row, at : at + 128]
                    gz_a = wide_ref[k, row, at + 128 : at + 256]
                    gz_b = wide_ref[k, row, at + 256 : at + 384]
                    a_up, b_up = pltpu.roll(a, 112, 1), pltpu.roll(b, 112, 1)
                    a_down, b_down = pltpu.roll(a, 16, 1), pltpu.roll(b, 16, 1)
                    yp = (jnp.where(lane < 112, a_up, b_up), jnp.where(lane < 112, b_up, gy))
                    ym = (jnp.where(lane < 16, gy, a_down), jnp.where(lane < 16, a_down, b_down))
                    zp = (
                        jnp.where(column == B - 1, gz_a, pltpu.roll(a, 127, 1)),
                        jnp.where(column == B - 1, gz_b, pltpu.roll(b, 127, 1)),
                    )
                    zm = (
                        jnp.where(column == 0, gz_a, pltpu.roll(a, 1, 1)),
                        jnp.where(column == 0, gz_b, pltpu.roll(b, 1, 1)),
                    )
                    for h, v in enumerate((a, b)):
                        cols = slice(128 * h, 128 * h + 128)
                        put_parts(
                            hi_ref.at[k],
                            lo_ref.at[k],
                            cols,
                            ((f * B, v), (ROWS + f * B, yp[h] - ym[h]), (2 * ROWS + f * B, zp[h] - zm[h])),
                        )
                        rest_ref[k, row, cols] = 0.25 * v + 0.125 * ((yp[h] + ym[h]) + (zp[h] + zm[h]))
                put_parts(
                    hi_ref.at[k], lo_ref.at[k], slice(None), ((3 * ROWS, face_out_ref[k, 32 * t : 32 * t + 32, :]),)
                )
            for k in range(BATCH):
                product(coef_ref, hi_ref.at[k], lo_ref.at[k], total_ref.at[k])
            for k in range(BATCH):
                for f in range(F):
                    row = slice(f * B, f * B + B)
                    value = rest_ref[k, row, :] + total_ref[k, row, :]
                    if t == 0:
                        value_ref[k, row, :] = value
                    else:
                        out_ref[first_slot + k, f] = jnp.where(sources[k] >= 0, value, 0.0)
                        hi, lo = split(value)
                        hi_ref[k, row, :] = hi
                        hi_ref[k, ROWS + f * B : ROWS + f * B + B, :] = lo
        write_out(i).start()
        for k in range(BATCH):
            mean_ref[k] = dot(hi_ref[k, 0:ROWS, :], pair_ref[...]) + dot(
                hi_ref[k, ROWS : 2 * ROWS, :], pair_ref[...]
            )
        for k in range(BATCH):

            @pl.when(sources[k] >= 0)
            def _():
                for f in range(F // 2):
                    halves = [
                        mean_ref[k, pl.ds(g * B, H, stride=2), :] + mean_ref[k, pl.ds(g * B + 1, H, stride=2), :]
                        for g in (f, f + F // 2)
                    ]
                    back_ref[sources[k], f * H : f * H + H, :] = jnp.where(
                        lane8 < 64, halves[0], pltpu.roll(halves[1], 64, 1)
                    )

        return 0

    lax.fori_loop(0, batches, batch, 0)

    def empty(i, _):
        for k in range(BATCH):
            out_ref[i * BATCH + k] = jnp.zeros(out_ref.shape[1:], F32)
        write_out(i).start()
        return 0

    lax.fori_loop(batches, FSLOTS // BATCH, empty, 0)
    for i in range(FSLOTS // BATCH):
        write_out(i).wait()


def place_kernel(owner_hbm, offset_hbm, new_ref, back_ref, out_ref, work_ref, sems, owner_ref, offset_ref):
    fetch_owner = fetch(owner_hbm, owner_ref, sems.at[B])
    fetch_offset = fetch(offset_hbm, offset_ref, sems.at[B + 1])
    for x in range(B):
        work_ref[x * PITCH : x * PITCH + ROWS, :] = new_ref[x * ROWS : (x + 1) * ROWS, :]
    fetch_owner.wait()
    fetch_offset.wait()
    lane = lanes_of((8, 128))

    def box(w, _):
        member, ox, oy, oz = box_place(owner_ref, offset_ref, w)
        z0 = w * B + oz
        inside = (lane >= z0) & (lane < z0 + H)
        pick = jnp.where(inside, lane - z0, 0)
        corner = ox * PITCH + oy
        for group in range(2):
            rows = [
                pl.ds(corner + (group * 5 + f) * B + y, H, stride=PITCH) for f in range(F // 2) for y in range(H)
            ]
            before = [work_ref[r, :] for r in rows]
            for f in range(F // 2):
                tile = back_ref[member, f * H : f * H + H, :]
                for y in range(H):
                    moved = jnp.take_along_axis(tile, pick + (group * 64 + y * 8), axis=1, mode="promise_in_bounds")
                    work_ref[rows[f * H + y], :] = jnp.where(inside, moved, before[f * H + y])
        return 0

    lax.fori_loop(0, BOXES, box, 0)
    copies = [
        pltpu.make_async_copy(
            work_ref.at[x * PITCH : x * PITCH + ROWS, :], out_ref.at[x * ROWS : (x + 1) * ROWS, :], sems.at[x]
        )
        for x in range(B)
    ]
    for copy in copies:
        copy.start()
    for copy in copies:
        copy.wait()


INDEX = [pltpu.SMEM((BOXES * LINES * GROUP,), jnp.int32), pltpu.SMEM((3, BOXES * LINES * GROUP), jnp.int32)]


def call(kernel, operands, outs, limit, scratch=(), hbm=(), hbm_outs=()):
    space = lambda cond: pl.BlockSpec(memory_space=pltpu.HBM if cond else pltpu.VMEM)
    return pl.pallas_call(
        kernel,
        in_specs=[space(i in hbm) for i in range(len(operands))],
        out_specs=[space(i in hbm_outs) for i in range(len(outs))],
        out_shape=[jax.ShapeDtypeStruct(*out) for out in outs],
        scratch_shapes=list(scratch),
        compiler_params=pltpu.CompilerParams(vmem_limit_bytes=limit * MIB),
    )(*operands)


def local(coarse_state, fine_state, flux_jacobians, fine_owner, fine_offset):
    rows = coarse_state.reshape(B * ROWS, 128)
    fine_rows = jnp.transpose(fine_state, (0, 2, 1, 3))
    offset = jnp.transpose(fine_offset, (1, 0))
    jacobians = jnp.transpose(flux_jacobians, (1, 0, 2))

    face = ((ROWS, 128), F32)
    x_first, x_last, y_first, y_last, z_first, z_last = call(faces_kernel, (rows,), [face] * 6, 4)

    def from_below(value, axis):
        n = lax.axis_size(axis)
        return lax.ppermute(value, axis, [(i, (i + 1) % n) for i in range(n)])

    def from_above(value, axis):
        n = lax.axis_size(axis)
        return lax.ppermute(value, axis, [((i + 1) % n, i) for i in range(n)])

    halo = (
        from_below(x_last, "gx"),
        from_above(x_first, "gx"),
        from_below(y_last, "gy"),
        from_above(y_first, "gy"),
        from_below(z_last, "gz"),
        from_above(z_first, "gz"),
    )
    new, outgoing, coef = call(
        coarse_kernel,
        (fine_owner, offset, rows, *halo, jacobians),
        [((B * ROWS, 128), F32), ((GROUP, MESSAGE, 128), F32), ((2, ROWS, 512), BF16)],
        14,
        [pltpu.VMEM((B * PITCH, 128), F32)] * 2
        + [pltpu.VMEM((B // 2, 512, 256), BF16)] * 2
        + [pltpu.VMEM((B // 2, ROWS, 256), F32)] * 2
        + [pltpu.VMEM((2, ROWS, 512), BF16), pltpu.VMEM((3, 16, 128), F32)]
        + INDEX
        + [pltpu.VMEM((F, 3, F), F32), pltpu.SemaphoreType.DMA((3,))],
        hbm=(0, 1, 9),
    )
    arrived = lax.all_to_all(outgoing, ("gx", "gy"), split_axis=0, concat_axis=0, tiled=True)

    fine_new, returning = call(
        fine_kernel,
        (fine_owner, fine_rows, arrived, coef),
        [((FSLOTS, F, B, 256), F32), ((GROUP, HALF // 2, 128), F32)],
        24,
        [pltpu.VMEM((BATCH, 512, 256), BF16)] * 2
        + [pltpu.VMEM((BATCH, ROWS, 768), F32)]
        + [pltpu.VMEM((BATCH, ROWS, 256), F32)] * 3
        + [
            pltpu.VMEM((BATCH, 64, 256), F32),
            pltpu.VMEM((BATCH, ROWS, 128), F32),
            pltpu.VMEM((BATCH, ROWS + 64, 128), BF16),
            pltpu.VMEM((BATCH, ROWS, 128), F32),
            pltpu.SMEM((FSLOTS + 1,), jnp.int32),
            INDEX[0],
            pltpu.VMEM((FSLOTS, F, B, 256), F32),
            pltpu.VMEM((FSLOTS, F, B, 256), F32),
            pltpu.VMEM((128, 768), BF16),
            pltpu.VMEM((128, 256), BF16),
            pltpu.VMEM((256, 128), BF16),
            pltpu.SemaphoreType.DMA((1 + 2 * (FSLOTS // BATCH),)),
        ],
        hbm=(0, 1),
        hbm_outs=(0,),
    )
    came_back = lax.all_to_all(returning, ("gx", "gy"), split_axis=0, concat_axis=0, tiled=True)

    coarse_out = call(
        place_kernel,
        (fine_owner, offset, new, came_back),
        [((B * ROWS, 128), F32)],
        4,
        [pltpu.VMEM((B * PITCH, 128), F32), pltpu.SemaphoreType.DMA((B + 2,))] + INDEX,
        hbm=(0, 1),
        hbm_outs=(0,),
    )[0]
    return coarse_out.reshape(coarse_state.shape), jnp.transpose(fine_new, (0, 2, 1, 3))


def solution(mesh):
    in_specs = (P("gx", None, "gy", "gz"), P(("gx", "gy", "gz"), None, None, None), P(), P(), P())
    out_specs = (P("gx", None, "gy", "gz"), P(("gx", "gy", "gz"), None, None, None))
    return jax.shard_map(local, mesh=mesh, in_specs=in_specs, out_specs=out_specs, check_vma=False)
```

```python
import functools

import jax
import jax.numpy as jnp
from jax import lax
from jax.experimental import pallas as pl
from jax.experimental.pallas import tpu as pltpu
from jax.sharding import PartitionSpec as P

F = 10
B = 16
BOXES = 8
H = 8
FSLOTS = 16
LINES = 8
GROUP = 16
ROWS = F * B
HALF = F * H
F32 = jnp.float32
BF16 = jnp.bfloat16
MESSAGE = HALF // 2 + 24
MIB = 1024 * 1024
PITCH = ROWS + 8
BATCH = 8


def dot(a, b):
    return jnp.dot(a, b, preferred_element_type=F32)


def split(v):
    hi = v.astype(BF16)
    return hi, (v - hi.astype(F32)).astype(BF16)


def lanes_of(shape):
    return lax.broadcasted_iota(jnp.int32, shape, len(shape) - 1)


def fine_constants(ghost_ref, face_ref, mean_ref):
    def one(cond):
        return jnp.where(cond, 1.0, 0.0).astype(BF16)

    row, col = (lax.broadcasted_iota(jnp.int32, (128, 384), d) for d in range(2))
    cell = col - 128
    y, z = cell // B, cell % B
    target = jnp.where(
        col < 16,
        col // 2,
        jnp.where(
            col < 112,
            -1,
            jnp.where(
                col < 128,
                8 + (col - 112) // 2,
                jnp.where(z == 0, 16 + y // 2, jnp.where(z == B - 1, 24 + y // 2, -1)),
            ),
        ),
    )
    for t in range(2):
        ghost_ref[:, 384 * t : 384 * t + 384] = one(row % 64 == target + jnp.where(target < 0, -64, 32 * t))
    row, col = (lax.broadcasted_iota(jnp.int32, (128, 256), d) for d in range(2))
    face_ref[...] = one(row % 64 == col // B // 2 * H + col % B // 2)
    row, col = (lax.broadcasted_iota(jnp.int32, (256, 128), d) for d in range(2))
    mean_ref[...] = one(col == row // B // 2 * H + row % B // 2) * jnp.asarray(0.125, BF16)


def device_index():
    return (lax.axis_index("gx") * lax.axis_size("gy") + lax.axis_index("gy")) * lax.axis_size("gz") + lax.axis_index("gz")


def box_place(owner_ref, offset_ref, w):
    box = device_index() * BOXES + w
    return (lax.shift_right_logical(owner_ref[box], 7), *(offset_ref[d, box] for d in range(3)))


def fetch(src, dst, sem):
    copy = pltpu.make_async_copy(src, dst, sem)
    copy.start()
    return copy


def coefficients(pad_ref, order, out):
    row, lane = (lax.broadcasted_iota(jnp.int32, (128, 128), d) for d in range(2))
    eye = jnp.where((row[:16] == lane[:16]) & (row[:16] < F), 0.125, 0.0).astype(F32)
    scaled = [0.125 * pad_ref[d] for d in range(3)]
    row, col = (lax.broadcasted_iota(jnp.int32, (128, 512), d) for d in range(2))
    block, inner = col // ROWS, col % ROWS // B
    ghost = 3 * ROWS
    target = jnp.where(col < ghost, inner + jnp.where(block == 0, 0, 16 + 16 * block), (col + 16) % 32)
    one = lambda cond: jnp.where(cond, 1.0, 0.0).astype(F32)
    first = one(row == target).astype(BF16)
    second = one((col < ROWS) & (row == 16 + inner)).astype(BF16)
    row, col = (lax.broadcasted_iota(jnp.int32, (ROWS, 512), d) for d in range(2))
    here, there = row % B, col % B
    edge = jnp.where(col < ghost + 16, 0, B - 1)
    distance = jnp.where(col < ROWS, there - here - 1, jnp.where(col < ghost, there - here, here - edge))
    mask_first = one(distance == 0)
    mask_second = one((col < ROWS) & (there + 1 == here))
    row, col = (lax.broadcasted_iota(jnp.int32, (ROWS, 128), d) for d in range(2))
    rows = one(row // B == col).astype(BF16)
    pad = jnp.zeros((112, 512), BF16)
    s, a, b = order
    coef = (
        (eye - scaled[s])
        + pltpu.roll(eye + scaled[s], 16, 1)
        - pltpu.roll(scaled[a], 32, 1)
        - pltpu.roll(scaled[b], 48, 1)
    )
    for part, value in enumerate(split(coef)):
        wide1 = jnp.concatenate([dot(value, first).astype(BF16), pad], axis=0)
        wide2 = jnp.concatenate([dot(value, second).astype(BF16), pad], axis=0)
        out[part] = (dot(rows, wide1) * mask_first + dot(rows, wide2) * mask_second).astype(BF16)


def prepare_kernel(pad_ref, coef_ref, ghost_ref, face_ref, mean_ref):
    coefficients(pad_ref, (0, 1, 2), coef_ref)
    fine_constants(ghost_ref, face_ref, mean_ref)


def faces_kernel(coarse_ref, x_lo, x_hi, y_lo, y_hi, z_lo, z_hi):
    x_lo[...] = coarse_ref[0:ROWS, :]
    x_hi[...] = coarse_ref[(B - 1) * ROWS : B * ROWS, :]
    for x in range(B):
        y_lo[x * F : x * F + F, :] = coarse_ref[pl.ds(x * ROWS, F, stride=B), :]
        y_hi[x * F : x * F + F, :] = coarse_ref[pl.ds(x * ROWS + B - 1, F, stride=B), :]
    lane = lanes_of((ROWS, 128))
    low = jnp.zeros((ROWS, 128), F32)
    high = jnp.zeros((ROWS, 128), F32)
    for x in range(B):
        plane = coarse_ref[x * ROWS : (x + 1) * ROWS, :]
        low = jnp.where(lane == x, pltpu.roll(plane, x, 1), low)
        high = jnp.where(lane == x, pltpu.roll(plane, x + 1, 1), high)
    z_lo[...] = low
    z_hi[...] = high


def product(coef_ref, hi_ref, lo_ref, total_ref):
    both = dot(coef_ref[...].reshape(2 * ROWS, 512), hi_ref[...])
    total_ref[...] = both[:ROWS] + both[ROWS:] + dot(coef_ref[0], lo_ref[...])


def put_parts(hi_ref, lo_ref, cols, parts):
    for at, value in parts:
        hi, lo = split(value)
        hi_ref[at : at + value.shape[0], cols] = hi
        lo_ref[at : at + value.shape[0], cols] = lo


def coarse_kernel(
    owner_hbm, offset_hbm, coarse_ref, x_lo, x_hi, y_lo, y_hi, z_lo, z_hi, jac_hbm, new_ref, out_ref, pad_ref, old_ref,
    mid_ref, hi_ref, lo_ref, rest_ref, total_ref, coef_ref,
    owner_ref, offset_ref, jac_ref, sems
):
    fetch_owner = fetch(owner_hbm, owner_ref, sems.at[0])
    fetch_offset = fetch(offset_hbm, offset_ref, sems.at[1])
    fetch(jac_hbm, jac_ref, sems.at[2]).wait()
    pad_ref[...] = jnp.zeros(pad_ref.shape, F32)
    for d in range(3):
        for g in range(F):
            pad_ref[d, g : g + 1, 0:F] = jac_ref[g, d : d + 1, :]
    coefficients(pad_ref, (1, 0, 2), coef_ref)
    lane = lanes_of((B, 128))
    ghost_zero = jnp.zeros((16 - F, 128), F32)
    for pair in range(B // 2):
        for side in range(2):
            x = 2 * pair + side
            cols = slice(side * 128, side * 128 + 128)
            for f in range(F):
                row = slice(f * B, f * B + B)
                here = x * ROWS + f * B
                p = coarse_ref[here : here + B, :]
                xm = coarse_ref[here - ROWS : here - ROWS + B, :] if x > 0 else x_lo[row, :]
                xp = coarse_ref[here + ROWS : here + ROWS + B, :] if x < B - 1 else x_hi[row, :]
                zm = jnp.where(lane == 0, pltpu.roll(z_lo[row, :], (128 - x) % 128, 1), pltpu.roll(p, 1, 1))
                zp = jnp.where(lane == 127, pltpu.roll(z_hi[row, :], 127 - x, 1), pltpu.roll(p, 127, 1))
                put_parts(
                    hi_ref.at[pair],
                    lo_ref.at[pair],
                    cols,
                    ((f * B, p), (ROWS + f * B, xp - xm), (2 * ROWS + f * B, zp - zm)),
                )
                rest_ref[pair, row, cols] = 0.25 * p + 0.125 * ((xp + xm) + (zp + zm))
                old_ref[x * PITCH + f * B : x * PITCH + f * B + B, :] = p
            low = jnp.concatenate([y_lo[x * F : x * F + F, :], ghost_zero], axis=0)
            high = jnp.concatenate([y_hi[x * F : x * F + F, :], ghost_zero], axis=0)
            put_parts(hi_ref.at[pair], lo_ref.at[pair], cols, ((3 * ROWS, low), (3 * ROWS + 16, high)))
    for pair in range(B // 2):
        product(coef_ref, hi_ref.at[pair], lo_ref.at[pair], total_ref.at[pair])
    for pair in range(B // 2):
        for side in range(2):
            x = 2 * pair + side
            cols = slice(side * 128, side * 128 + 128)
            for f in range(F):
                row = slice(f * B, f * B + B)
                here = slice(x * ROWS + f * B, x * ROWS + f * B + B)
                new = rest_ref[pair, row, cols] + total_ref[pair, row, cols]
                new_ref[here, :] = new
                mid_ref[x * PITCH + f * B : x * PITCH + f * B + B, :] = 0.5 * (coarse_ref[here, :] + new)

    fetch_owner.wait()
    fetch_offset.wait()
    lane8 = lanes_of((8, 128))
    within = lane8 % 32
    base = jnp.where(within < 16, within % 8, jnp.where(within < 24, -1, 8))
    window = lane8 % 8

    def box(w, _):
        member, ox, oy, oz = box_place(owner_ref, offset_ref, w)
        z0 = w * B + oz
        pick = base + z0
        pick_x = window + z0
        corner = ox * PITCH + oy - 1
        for f in range(F // 2):
            acc = jnp.zeros((8, 128), F32)
            for half in range(2):
                for t, ref in enumerate((old_ref, mid_ref)):
                    low = 64 * half + 32 * t
                    for y in range(H + 2):
                        rows = ref[pl.ds(corner + (f + 5 * half) * B + y, H, stride=PITCH), :]
                        moved = jnp.take_along_axis(rows, pick, axis=1, mode="promise_in_bounds")
                        if y == 0:
                            put = (lane8 >= low) & (lane8 < low + 8)
                        elif y == H + 1:
                            put = (lane8 >= low + 8) & (lane8 < low + 16)
                        else:
                            put = (lane8 == low + 15 + y) | (lane8 == low + 23 + y)
                        acc = jnp.where(put, moved, acc)
            out_ref[member, f * 8 : f * 8 + 8, :] = acc
        tiles = [jnp.zeros((8, 128), F32)] * 3
        for side, x in enumerate((ox - 1, ox + H)):
            for y in range(H):
                low = 64 * side + 8 * y
                put = (lane8 >= low) & (lane8 < low + 8)
                at = x * PITCH + oy + y
                tails = [ref[pl.ds(at + 8 * B, F - 8, stride=B), :] for ref in (old_ref, mid_ref)]
                values = [ref[pl.ds(at, 8, stride=B), :] for ref in (old_ref, mid_ref)]
                values.append(jnp.concatenate(tails + [jnp.zeros((4, 128), F32)], axis=0))
                for n, value in enumerate(values):
                    moved = jnp.take_along_axis(value, pick_x, axis=1, mode="promise_in_bounds")
                    tiles[n] = jnp.where(put, moved, tiles[n])
        for n in range(3):
            out_ref[member, HALF // 2 + 8 * n : HALF // 2 + 8 * n + 8, :] = tiles[n]
        return 0

    lax.fori_loop(0, BOXES, box, 0, unroll=2)


def fine_kernel(
    owner_hbm, fine_hbm, arrived_ref, coef_ref, ghost_ref, face_ref, pair_ref, out_hbm, back_ref, hi_ref, lo_ref, wide_ref, rest_ref,
    total_ref, value_ref, face_out_ref, spread_ref, mixed_ref, mean_ref, source_ref, owner_ref, fine_ref, out_ref,
    sems
):
    fetch_owner = fetch(owner_hbm, owner_ref, sems.at[0])
    batches_at = [slice(i * BATCH, i * BATCH + BATCH) for i in range(FSLOTS // BATCH)]
    fetch_fine = [fetch(fine_hbm.at[at], fine_ref.at[at], sems.at[1 + i]) for i, at in enumerate(batches_at)]
    for slot in range(FSLOTS):
        source_ref[slot] = -1
    first_here = device_index() * FSLOTS
    line = lax.axis_index("gz")
    fetch_owner.wait()
    for member in range(GROUP):
        for w in range(BOXES):
            holder = owner_ref[(member * LINES + line) * BOXES + w]
            source_ref[jnp.minimum(holder ^ first_here, FSLOTS)] = member
    held = sum(jnp.where(source_ref[slot] >= 0, 1, 0) for slot in range(FSLOTS))
    batches = (held + BATCH - 1) // BATCH
    for copy in fetch_fine:
        copy.wait()

    def write_out(i):
        at = pl.ds(i * BATCH, BATCH)
        return pltpu.make_async_copy(out_ref.at[at], out_hbm.at[at], sems.at[3 + i])

    def batch(i, _):
        first_slot = i * BATCH
        sources = [source_ref[first_slot + k] for k in range(BATCH)]
        lane = lanes_of((B, 128))
        column = lane % B
        lane8 = lanes_of((8, 128))
        for k in range(BATCH):
            message = arrived_ref.at[jnp.maximum(sources[k], 0)]
            tail = message[MESSAGE - 8 : MESSAGE, :]
            for t in range(2):
                at = HALF // 2 + 8 * t
                value = jnp.concatenate([message[at : at + 8, :], pltpu.roll(tail, 6, 0) if t else tail], axis=0)
                hi = value.astype(BF16).astype(F32)
                lo = pltpu.roll(value - hi, 64, 1)
                at = ROWS + 32 * t
                mixed_ref[k, at : at + 16, :] = jnp.where(lane < 64, hi, lo).astype(BF16)
                mixed_ref[k, at + 16 : at + 32, :] = jnp.where(lane < 64, lo, hi).astype(BF16)
            for f in range(F):
                value = message[f % 5 * H : f % 5 * H + H, :]
                hi = value.astype(BF16).astype(F32)
                lo = pltpu.roll(value - hi, 64, 1)
                both = jnp.where(lane8 < 64, hi, lo) if f < 5 else jnp.where(lane8 < 64, lo, hi)
                spread_ref[k, pl.ds(f * B, H, stride=2), :] = both
                spread_ref[k, pl.ds(f * B + 1, H, stride=2), :] = both
        for k in range(BATCH):
            for f in range(F):
                row = slice(f * B, f * B + B)
                mixed_ref[k, row, :] = spread_ref[k, row, :].astype(BF16)
        for k in range(BATCH):
            wide_ref[k] = dot(mixed_ref[k, 0:ROWS, :], ghost_ref[...])
            face_out_ref[k] = dot(mixed_ref[k, ROWS : ROWS + 64, :], face_ref[...])
        for t in range(2):
            at = 384 * t
            for k in range(BATCH):
                for f in range(F):
                    row = slice(f * B, f * B + B)
                    if t == 0:
                        a, b = fine_ref[first_slot + k, f, :, 0:128], fine_ref[first_slot + k, f, :, 128:256]
                    else:
                        a, b = value_ref[k, row, 0:128], value_ref[k, row, 128:256]
                    gy = wide_ref[k, row, at : at + 128]
                    gz_a = wide_ref[k, row, at + 128 : at + 256]
                    gz_b = wide_ref[k, row, at + 256 : at + 384]
                    a_up, b_up = pltpu.roll(a, 112, 1), pltpu.roll(b, 112, 1)
                    a_down, b_down = pltpu.roll(a, 16, 1), pltpu.roll(b, 16, 1)
                    yp = (jnp.where(lane < 112, a_up, b_up), jnp.where(lane < 112, b_up, gy))
                    ym = (jnp.where(lane < 16, gy, a_down), jnp.where(lane < 16, a_down, b_down))
                    zp = (
                        jnp.where(column == B - 1, gz_a, pltpu.roll(a, 127, 1)),
                        jnp.where(column == B - 1, gz_b, pltpu.roll(b, 127, 1)),
                    )
                    zm = (
                        jnp.where(column == 0, gz_a, pltpu.roll(a, 1, 1)),
                        jnp.where(column == 0, gz_b, pltpu.roll(b, 1, 1)),
                    )
                    for h, v in enumerate((a, b)):
                        cols = slice(128 * h, 128 * h + 128)
                        put_parts(
                            hi_ref.at[k],
                            lo_ref.at[k],
                            cols,
                            ((f * B, v), (ROWS + f * B, yp[h] - ym[h]), (2 * ROWS + f * B, zp[h] - zm[h])),
                        )
                        rest_ref[k, row, cols] = 0.25 * v + 0.125 * ((yp[h] + ym[h]) + (zp[h] + zm[h]))
                put_parts(
                    hi_ref.at[k], lo_ref.at[k], slice(None), ((3 * ROWS, face_out_ref[k, 32 * t : 32 * t + 32, :]),)
                )
            for k in range(BATCH):
                product(coef_ref, hi_ref.at[k], lo_ref.at[k], total_ref.at[k])
            for k in range(BATCH):
                for f in range(F):
                    row = slice(f * B, f * B + B)
                    value = rest_ref[k, row, :] + total_ref[k, row, :]
                    if t == 0:
                        value_ref[k, row, :] = value
                    else:
                        out_ref[first_slot + k, f] = jnp.where(sources[k] >= 0, value, 0.0)
                        hi, lo = split(value)
                        hi_ref[k, row, :] = hi
                        hi_ref[k, ROWS + f * B : ROWS + f * B + B, :] = lo
        write_out(i).start()
        for k in range(BATCH):
            mean_ref[k] = dot(hi_ref[k, 0:ROWS, :], pair_ref[...]) + dot(
                hi_ref[k, ROWS : 2 * ROWS, :], pair_ref[...]
            )
        for k in range(BATCH):

            @pl.when(sources[k] >= 0)
            def _():
                for f in range(F // 2):
                    halves = [
                        mean_ref[k, pl.ds(g * B, H, stride=2), :] + mean_ref[k, pl.ds(g * B + 1, H, stride=2), :]
                        for g in (f, f + F // 2)
                    ]
                    back_ref[sources[k], f * H : f * H + H, :] = jnp.where(
                        lane8 < 64, halves[0], pltpu.roll(halves[1], 64, 1)
                    )

        return 0

    lax.fori_loop(0, batches, batch, 0)

    def empty(i, _):
        for k in range(BATCH):
            out_ref[i * BATCH + k] = jnp.zeros(out_ref.shape[1:], F32)
        write_out(i).start()
        return 0

    lax.fori_loop(batches, FSLOTS // BATCH, empty, 0)
    for i in range(FSLOTS // BATCH):
        write_out(i).wait()


def place_kernel(owner_hbm, offset_hbm, new_ref, back_ref, out_ref, work_ref, sems, owner_ref, offset_ref):
    fetch_owner = fetch(owner_hbm, owner_ref, sems.at[B])
    fetch_offset = fetch(offset_hbm, offset_ref, sems.at[B + 1])
    for x in range(B):
        work_ref[x * PITCH : x * PITCH + ROWS, :] = new_ref[x * ROWS : (x + 1) * ROWS, :]
    fetch_owner.wait()
    fetch_offset.wait()
    lane = lanes_of((8, 128))

    def box(w, _):
        member, ox, oy, oz = box_place(owner_ref, offset_ref, w)
        z0 = w * B + oz
        inside = (lane >= z0) & (lane < z0 + H)
        pick = jnp.where(inside, lane - z0, 0)
        corner = ox * PITCH + oy
        for group in range(2):
            rows = [
                pl.ds(corner + (group * 5 + f) * B + y, H, stride=PITCH) for f in range(F // 2) for y in range(H)
            ]
            before = [work_ref[r, :] for r in rows]
            for f in range(F // 2):
                tile = back_ref[member, f * H : f * H + H, :]
                for y in range(H):
                    moved = jnp.take_along_axis(tile, pick + (group * 64 + y * 8), axis=1, mode="promise_in_bounds")
                    work_ref[rows[f * H + y], :] = jnp.where(inside, moved, before[f * H + y])
        return 0

    lax.fori_loop(0, BOXES, box, 0)
    copies = [
        pltpu.make_async_copy(
            work_ref.at[x * PITCH : x * PITCH + ROWS, :], out_ref.at[x * ROWS : (x + 1) * ROWS, :], sems.at[x]
        )
        for x in range(B)
    ]
    for copy in copies:
        copy.start()
    for copy in copies:
        copy.wait()


INDEX = [pltpu.SMEM((BOXES * LINES * GROUP,), jnp.int32), pltpu.SMEM((3, BOXES * LINES * GROUP), jnp.int32)]


def call(kernel, operands, outs, limit, scratch=(), hbm=(), hbm_outs=()):
    space = lambda cond: pl.BlockSpec(memory_space=pltpu.HBM if cond else pltpu.VMEM)
    return pl.pallas_call(
        kernel,
        in_specs=[space(i in hbm) for i in range(len(operands))],
        out_specs=[space(i in hbm_outs) for i in range(len(outs))],
        out_shape=[jax.ShapeDtypeStruct(*out) for out in outs],
        scratch_shapes=list(scratch),
        compiler_params=pltpu.CompilerParams(vmem_limit_bytes=limit * MIB),
    )(*operands)


def local(coarse_state, fine_state, flux_jacobians, fine_owner, fine_offset):
    rows = coarse_state.reshape(B * ROWS, 128)
    fine_rows = jnp.transpose(fine_state, (0, 2, 1, 3))
    offset = jnp.transpose(fine_offset, (1, 0))
    jacobians = jnp.transpose(flux_jacobians, (1, 0, 2))

    face = ((ROWS, 128), F32)
    x_first, x_last, y_first, y_last, z_first, z_last = call(faces_kernel, (rows,), [face] * 6, 4)

    def from_below(value, axis):
        n = lax.axis_size(axis)
        return lax.ppermute(value, axis, [(i, (i + 1) % n) for i in range(n)])

    def from_above(value, axis):
        n = lax.axis_size(axis)
        return lax.ppermute(value, axis, [((i + 1) % n, i) for i in range(n)])

    halo = (
        from_below(x_last, "gx"),
        from_above(x_first, "gx"),
        from_below(y_last, "gy"),
        from_above(y_first, "gy"),
        from_below(z_last, "gz"),
        from_above(z_first, "gz"),
    )
    new, outgoing, padded = call(
        coarse_kernel,
        (fine_owner, offset, rows, *halo, jacobians),
        [((B * ROWS, 128), F32), ((GROUP, MESSAGE, 128), F32), ((3, 16, 128), F32)],
        14,
        [pltpu.VMEM((B * PITCH, 128), F32)] * 2
        + [pltpu.VMEM((B // 2, 512, 256), BF16)] * 2
        + [pltpu.VMEM((B // 2, ROWS, 256), F32)] * 2
        + [pltpu.VMEM((2, ROWS, 512), BF16)]
        + INDEX
        + [pltpu.VMEM((F, 3, F), F32), pltpu.SemaphoreType.DMA((3,))],
        hbm=(0, 1, 9),
    )
    prepared = call(
        prepare_kernel,
        (padded,),
        [((2, ROWS, 512), BF16), ((128, 768), BF16), ((128, 256), BF16), ((256, 128), BF16)],
        6,
    )
    arrived = lax.all_to_all(outgoing, ("gx", "gy"), split_axis=0, concat_axis=0, tiled=True)

    fine_new, returning = call(
        fine_kernel,
        (fine_owner, fine_rows, arrived, *prepared),
        [((FSLOTS, F, B, 256), F32), ((GROUP, HALF // 2, 128), F32)],
        24,
        [pltpu.VMEM((BATCH, 512, 256), BF16)] * 2
        + [pltpu.VMEM((BATCH, ROWS, 768), F32)]
        + [pltpu.VMEM((BATCH, ROWS, 256), F32)] * 3
        + [
            pltpu.VMEM((BATCH, 64, 256), F32),
            pltpu.VMEM((BATCH, ROWS, 128), F32),
            pltpu.VMEM((BATCH, ROWS + 64, 128), BF16),
            pltpu.VMEM((BATCH, ROWS, 128), F32),
            pltpu.SMEM((FSLOTS + 1,), jnp.int32),
            INDEX[0],
            pltpu.VMEM((FSLOTS, F, B, 256), F32),
            pltpu.VMEM((FSLOTS, F, B, 256), F32),
            pltpu.SemaphoreType.DMA((1 + 2 * (FSLOTS // BATCH),)),
        ],
        hbm=(0, 1),
        hbm_outs=(0,),
    )
    came_back = lax.all_to_all(returning, ("gx", "gy"), split_axis=0, concat_axis=0, tiled=True)

    coarse_out = call(
        place_kernel,
        (fine_owner, offset, new, came_back),
        [((B * ROWS, 128), F32)],
        4,
        [pltpu.VMEM((B * PITCH, 128), F32), pltpu.SemaphoreType.DMA((B + 2,))] + INDEX,
        hbm=(0, 1),
        hbm_outs=(0,),
    )[0]
    return coarse_out.reshape(coarse_state.shape), jnp.transpose(fine_new, (0, 2, 1, 3))


def solution(mesh):
    in_specs = (P("gx", None, "gy", "gz"), P(("gx", "gy", "gz"), None, None, None), P(), P(), P())
    out_specs = (P("gx", None, "gy", "gz"), P(("gx", "gy", "gz"), None, None, None))
    return jax.shard_map(local, mesh=mesh, in_specs=in_specs, out_specs=out_specs, check_vma=False)
```
